32 devices in a mesh: seq: 8 (over z, x), exp: 4 (over y, core).
Axes of the slice: x: 2, y: 2, z: 4, core: 2. Of those that a mesh axis runs over, the one named last changes fastest.
Arguments:
- tokens: bfloat16 [24576, 512], P(('seq', 'exp')), may hold values from -6 to 6
- lengths: int32 [8, 4], P('seq'), may hold values from 1 to 2688, 3072 in all within a row
- routes: int32 [24576, 4], P(('seq', 'exp')), may hold values from 0 to 11, all different within a row; in each aligned block of 768 rows (0 to 767, 768 to 1535, ...) at most 384 rows name the same one
- gates: float32 [24576, 4], P(('seq', 'exp')), may hold values from 0.1 to 0.4
- gain_attn: float32 [512], replicated, may hold values from 0.25 to 1.75
- w_kv: bfloat16 [512, 128], replicated, may hold values from -0.25 to 0.25
- w_query: bfloat16 [12, 512, 64], P('exp'), may hold values from -0.5 to 0.5
- w_out: bfloat16 [12, 64, 512], P('exp'), may hold values from -6 to 6
- gain_ffn: float32 [512], replicated, may hold values from 0.25 to 1.75
- w_up: bfloat16 [512, 2048], replicated, may hold values from -0.25 to 0.25
- w_down: bfloat16 [2048, 512], replicated, may hold values from -0.125 to 0.125
- cotangent: bfloat16 [24576, 512], P(('seq', 'exp')), may hold values from -6 to 6
Outputs:
- block_out: bfloat16 [24576, 512], P(('seq', 'exp'))
- grad_tokens: bfloat16 [24576, 512], P(('seq', 'exp'))
- grad_gain_attn: float32 [512], replicated
- grad_kv: float32 [512, 128], replicated
- grad_query: float32 [12, 512, 64], P('exp')
- grad_out: float32 [12, 64, 512], P('exp')
- grad_gain_ffn: float32 [512], replicated
- grad_up: float32 [512, 2048], replicated
- grad_down: float32 [2048, 512], replicated
The draws below stay inside these ranges and needn't reach their ends.
Inputs may be any that keep to these rules, and one draw needn't show every extreme that they name: `routes`: each row names 4 different experts. Among the rows of one device, at most 384 name any one expert, a bound that some block reaches of them. The 4 lengths of a group add up to 3072; the longest has 2688 tokens.
All inputs are finite; a program needn't handle non-finite values.
Results may differ from the reference program's by a relative error of at most 0.015.
The reference program's roundings to bfloat16 on the way count: a program that leaves them out, or rounds other values in their place, can miss the bound.
Values may be sent and summed in bfloat16 or wider, within the bound.
A program may use at most 128 MiB of HBM per device.

```python
import math
import jax
import jax.numpy as jnp
import numpy as np
from jax import lax

D = 512
HS = 64
FF = 2048
TOPK = 4
DOCS = 4
TOK_DEV = 768
CAP = 384
EXPERTS = 12
GROUP_TOK = 3072
GROUPS = 8
TOKENS = 24576


def block_levels(own_key, shape, cuts, low, top_value):
    loudness = 1.0
    for position, parts in cuts:
        steps = jax.random.uniform(jax.random.fold_in(jax.random.fold_in(own_key, 6), position), (parts,), jnp.float32, low / len(cuts), top_value / len(cuts))
        loudness = loudness * jnp.repeat(jnp.exp(steps), shape[position] // parts).reshape((-1,) + (1,) * (len(shape) - 1 - position))
    return loudness


def split_up(amount, total, limit, lean):
    loads = [(1 << 20) // math.isqrt(standing ** lean) + 1 for standing in range(2, amount + 1)]
    spare, holding = total - limit - (amount - 1), [1] * (amount - 1)
    while spare > 0:
        movable = [i for i in range(amount - 1) if holding[i] < limit]
        whole, budget = sum([loads[i] for i in movable]), spare
        for i in movable:
            more = min(limit - holding[i], max(1, budget * loads[i] // whole), spare)
            holding[i] = holding[i] + more
            spare = spare - more
    return np.array([limit] + holding)


def uneven_parts(own_key, number_of, total, limit, lean):
    if number_of == 2:
        one = jax.random.randint(own_key, (), max(1, total - limit), min(limit, total - 1) + 1)
        return jnp.stack([one, total - one])
    tallies = jnp.asarray(split_up(number_of, total, limit, lean), jnp.int32)
    pairs = (number_of - 1) // 2
    source_of, receiver = tallies[1:1 + 2 * pairs:2], tallies[2:2 + 2 * pairs:2]
    slack = jnp.minimum(source_of - 1, limit - receiver)
    passed = jax.random.randint(jax.random.fold_in(own_key, 1), (pairs,), 0, 1 << 20) % (slack + 1)
    tallies = tallies.at[1:1 + 2 * pairs:2].set(source_of - passed).at[2:2 + 2 * pairs:2].set(receiver + passed)
    return tallies[jax.random.permutation(jax.random.fold_in(own_key, 2), number_of)]


def shared_out(stream_key, own, number, rows, amount, top, most, slope):
    order = jax.random.permutation(stream_key, amount)
    crowded, usual = load_shares(amount, rows * top, most, slope, True), load_shares(amount, rows * top, most, slope, False)
    places = jnp.arange(amount)

    def named(tallies, offset_by):
        used = int((tallies > 0).sum())
        fixed = max(1, used // 4)
        shifted = fixed + (places - fixed + offset_by * (used - fixed)) % max(1, amount - fixed)
        return jnp.zeros((amount,), jnp.int32).at[order[jnp.where(places < fixed, places, shifted)]].set(jnp.asarray(tallies, jnp.int32))

    tallies = jnp.where(number % 4 == 0, named(crowded, number // 4), named(usual, number - number // 4 - 1))
    mixed = jax.random.permutation(jax.random.fold_in(own, 3), amount)
    giver, receiver = mixed[0:amount // 2 * 2:2], mixed[1:amount // 2 * 2:2]
    room = jnp.minimum(tallies[giver] - 1, most - tallies[receiver]) // 2
    room = jnp.where((giver == order[0]) | (receiver == order[0]) | (tallies[receiver] == 0), 0, jnp.maximum(room, 0))
    shifted = jax.random.randint(jax.random.fold_in(own, 4), (amount // 2,), 0, 1 << 20) % (room + 1)
    tallies = tallies.at[giver].add(-shifted).at[receiver].add(shifted)
    items = jnp.searchsorted(jnp.cumsum(tallies), jnp.arange(rows * top), side="right").astype(jnp.int32)
    listing = items.reshape(top, rows).T
    listing = listing[jax.random.permutation(jax.random.fold_in(own, 1), rows)]
    offset_by = jax.random.randint(jax.random.fold_in(own, 2), (rows, 1), 0, top)
    return jnp.take_along_axis(listing, (jnp.arange(top)[None, :] + offset_by) % top, axis=1)


def load_shares(amount, total, reach, skew, full):
    portions = [(1 << 20) // math.isqrt(rank ** skew) + 1 for rank in range(1, amount + 1)]
    largest = reach if full else min(reach, max(-(-total // amount), total * portions[0] // sum(portions)))
    least = 1 if total - largest >= amount - 1 else 0
    given, rest = [largest] + [least] * (amount - 1), total - largest - least * (amount - 1)
    while rest > 0:
        movable = [i for i in range(1, amount) if given[i] < largest] or [i for i in range(1, amount) if given[i] < reach]
        whole, budget = sum([portions[i] for i in movable]), rest
        for i in movable:
            addition = min(reach - given[i], max(1, budget * portions[i] // whole), rest)
            given[i] = given[i] + addition
            rest = rest - addition
    return np.array(given)


def centred(key, extent, deviation, reach, cuts=(), kind=jnp.bfloat16):
    array = jax.random.normal(key, extent, jnp.float32) * deviation
    if len(cuts) > 0:
        array = block_levels(key, extent, cuts, -0.22, 0.18) * array
    return jnp.clip(array, min=-reach, max=reach).astype(kind)


def setup_inputs(seed: int = 0) -> dict:
    splits = jax.random.split(jax.random.key(seed), 13)
    tokens = centred(splits[0], (TOKENS, D), 1.0, 6.0, ((0, 32),))
    lengths = jax.vmap(lambda own: uneven_parts(own, DOCS, GROUP_TOK, GROUP_TOK - TOK_DEV // 2, 0))(jax.random.split(splits[1], GROUPS)).reshape((GROUPS, DOCS)).astype(jnp.int32)
    routes_keys = jax.random.split(jax.random.fold_in(splits[2], 1), TOKENS // TOK_DEV)
    routes_turns = jax.random.permutation(jax.random.fold_in(splits[2], 3), TOKENS // TOK_DEV)
    routes = jax.vmap(lambda own, number: shared_out(jax.random.fold_in(splits[2], 2), own, number, TOK_DEV, EXPERTS, TOPK, CAP, 2))(routes_keys, routes_turns).reshape((TOKENS, TOPK))
    gates = jnp.clip(0.1 + 0.3 * jax.random.uniform(splits[3], (TOKENS, TOPK), jnp.float32) ** block_levels(splits[3], (TOKENS, TOPK), ((0, 32),), -0.2, 0.2), 0.1, 0.4)
    gain_attn = jnp.clip(1.0 + 0.15 * jax.random.normal(splits[4], (D,), jnp.float32), 0.25, 1.75)
    w_kv = centred(splits[5], (D, 2 * HS), D ** -0.5, 0.25)
    w_query = centred(splits[6], (EXPERTS, D, HS), (D // 4) ** -0.5, 0.5, ((0, 4),))
    w_out = centred(splits[7], (EXPERTS, HS, D), 1.0, 6.0, ((0, 4),))
    gain_ffn = jnp.clip(1.0 + 0.15 * jax.random.normal(splits[8], (D,), jnp.float32), 0.25, 1.75)
    w_up = centred(splits[9], (D, FF), D ** -0.5, 0.25)
    w_down = centred(splits[10], (FF, D), FF ** -0.5, 0.125)
    cotangent = centred(splits[11], (TOKENS, D), 1.0, 6.0, ((0, 32),))
    return {"tokens": tokens, "lengths": lengths, "routes": routes, "gates": gates, "gain_attn": gain_attn, "w_kv": w_kv, "w_query": w_query, "w_out": w_out, "gain_ffn": gain_ffn, "w_up": w_up, "w_down": w_down, "cotangent": cotangent}


@jax.custom_vjp
def low(v):
    return lax.optimization_barrier(v.astype(jnp.bfloat16)).astype(jnp.float32)

@jax.custom_vjp
def low_back(v):
    return v

def low_keep(v):
    return (low(v), None)

def low_pass(kept, grad):
    return (grad,)

def back_keep(v):
    return (v, None)

def back_low(kept, grad):
    return (low(grad),)
low.defvjp(low_keep, low_pass)
low_back.defvjp(back_keep, back_low)
NORM_EPSILON = 1e-06
MASKED_SCORE = -1e+30
TOP_PRECISION = lax.Precision.HIGHEST

def rms_scale(values, gain_row):
    return values * lax.rsqrt(lax.optimization_barrier(jnp.mean(values * values, axis=-1, keepdims=True)) + NORM_EPSILON) * gain_row

def doc_index(positions, doc_ends):
    return lax.optimization_barrier(jnp.sum((positions[:, None] >= doc_ends[None, :]).astype(jnp.int32), axis=1)).astype(jnp.int32)

def attend_block(key_rows, value_rows, key_doc, doc_ends, query_block, pos_block):
    scores = low_back(jnp.dot(query_block, key_rows.T, precision=TOP_PRECISION) * (1.0 / math.sqrt(HS)))
    key_pos = jnp.arange(key_rows.shape[0], dtype=jnp.int32)
    allowed = (key_pos[None, :] <= pos_block[:, None]) & (key_doc[None, :] == doc_index(pos_block, doc_ends)[:, None])
    scores = jnp.where(allowed, scores, MASKED_SCORE)
    weights_row = low(jax.nn.softmax(scores, axis=-1))
    return jnp.dot(weights_row, value_rows, precision=TOP_PRECISION)

def group_forward(group_input, gain_attn, w_kv, w_query, w_out, gain_ffn, w_up, w_down, route_ids, gate_rows, doc_lengths):
    row_count = group_input.shape[0]
    doc_ends = jnp.cumsum(doc_lengths).astype(jnp.int32)
    positions = jnp.arange(row_count, dtype=jnp.int32)
    key_doc = doc_index(positions, doc_ends)
    normed = low(rms_scale(group_input, gain_attn))
    keyvalue = low_back(low(jnp.dot(normed, w_kv, precision=TOP_PRECISION)))
    key_rows = keyvalue[:, :HS]
    value_rows = keyvalue[:, HS:]
    route_hits = (route_ids[:, :, None] == jnp.arange(EXPERTS, dtype=jnp.int32)[None, None, :]).astype(jnp.float32)
    copies = low_back(jnp.broadcast_to(normed[:, None, :], (row_count, TOPK, D)))
    table_q = jnp.transpose(w_query, (1, 0, 2)).reshape(D, EXPERTS * HS)
    route_rows = row_count * TOPK
    every_query = jnp.dot(copies.reshape(route_rows, D), table_q, precision=TOP_PRECISION).reshape(row_count, TOPK, EXPERTS, HS)
    queries = low_back(low(lax.optimization_barrier(jnp.sum(route_hits[:, :, :, None] * every_query, axis=2))))
    block_rows = math.gcd(512, route_rows)
    query_blocks = queries.reshape(route_rows // block_rows, block_rows, HS)
    pos_blocks = jnp.repeat(positions, TOPK).reshape(route_rows // block_rows, block_rows)
    step_fn = jax.checkpoint(attend_block)
    attended = lax.map(lambda block_pair: step_fn(key_rows, value_rows, key_doc, doc_ends, block_pair[0], block_pair[1]), (query_blocks, pos_blocks))
    attended = low_back(low(attended.reshape(row_count, TOPK, HS)))
    spread = (route_hits[:, :, :, None] * attended[:, :, None, :]).reshape(route_rows, EXPERTS * HS)
    branch = low_back(low(jnp.dot(spread, w_out.reshape(EXPERTS * HS, D), precision=TOP_PRECISION))).reshape(row_count, TOPK, D)
    mixed_rows = group_input + lax.optimization_barrier(jnp.sum(gate_rows[:, :, None] * branch, axis=1))
    normed_ffn = low(rms_scale(mixed_rows, gain_ffn))
    hidden = low_back(jnp.dot(normed_ffn, w_up, precision=TOP_PRECISION))
    active = low(jax.nn.gelu(hidden))
    return mixed_rows + jnp.dot(active, w_down, precision=TOP_PRECISION)

def reference(tokens, lengths, routes, gates, gain_attn, w_kv, w_query, w_out, gain_ffn, w_up, w_down, cotangent):
    weights = tuple((weight.astype(jnp.float32) for weight in (gain_attn, w_kv, w_query, w_out, gain_ffn, w_up, w_down)))
    token_groups = tokens.astype(jnp.float32).reshape(GROUPS, GROUP_TOK, D)
    cot_groups = cotangent.astype(jnp.float32).reshape(GROUPS, GROUP_TOK, D)
    route_groups = routes.reshape(GROUPS, GROUP_TOK, TOPK)
    gate_groups = gates.astype(jnp.float32).reshape(GROUPS, GROUP_TOK, TOPK)

    def one_group(totals, group_pack):
        group_tokens, group_cot, group_routes, group_gates, group_lengths = group_pack

        def forward(group_input, *params):
            return group_forward(group_input, *params, group_routes, group_gates, group_lengths)
        result, pullback = jax.vjp(forward, group_tokens, *weights)
        all_grads = pullback(group_cot)
        totals = tuple((first + second for first, second in zip(totals, all_grads[1:])))
        return (totals, (result.astype(jnp.bfloat16), all_grads[0].astype(jnp.bfloat16)))
    zero_sums = tuple((jnp.zeros_like(weight) for weight in weights))
    totals, (results, grad_rows) = lax.scan(one_group, zero_sums, (token_groups, cot_groups, route_groups, gate_groups, lengths))
    return (results.reshape(TOKENS, D), grad_rows.reshape(TOKENS, D), totals[0], totals[1], totals[2], totals[3], totals[4], totals[5], totals[6])
```

```python
import functools
import math
import types
import typing

import jax
import jax.numpy as jnp
from jax import lax
from jax.experimental import pallas as pl
from jax.experimental.pallas import tpu as pltpu
from jax.sharding import PartitionSpec as P

NORM_EPSILON = 1e-06
MASKED_SCORE = -1e30
TILE_TOKENS = 256
QUERY, KEYS, OUT = range(3)
FF_CHUNK = 512
FINISH_STEPS = 4
CORE, Y, X, Z0, Z1 = ((1, 0), (1, 1), (0, 0), (0, 1), (0, 2))
Y_FIRST = (CORE, Y, X, Z0, Z1)
X_FIRST = (CORE, X, Y, Z0, Z1)
Z_FIRST = (CORE, Z0, Z1, Y, X)
FFN_SUMS = (
    (Y_FIRST, (1, 1, 1, 2), 0, (1, 1, 1, 2)),
    (Y_FIRST, (1, 2, 2), 0, (1, 2, 2)),
    (Z_FIRST, (1, 2, 2), 0, (1, 2, 2)),
    (Y_FIRST, (1, 2, 2), 0, (1, 1, 1, 2)),
)
OUT_SUMS = (Y_FIRST, (1, 1, 1, 2), 2, (1, 2))
QUERY_SUMS = (Y_FIRST, (1, 1, 1, 2), 2, (3,))
SMALL_SUMS = (Y_FIRST, (1, 2, 2), 0, (1, 2, 2))
SCHEDULE = {
    (0, 2): (0,),
    (0, 4): (1,),
    (0, 6): (2,),
    (1, 1): (0, 3),
    (2, 0): (4,),
    (2, 1): (1,),
    (2, 2): (0,),
    (2, 4): (2,),
    (2, 5): (3, 1),
    (2, 6): (4, 0),
    (2, 7): (2,),
    (2, 8): (3,),
    (3, 0): (4,),
    (3, 1): (1,),
    (3, 2): (2,),
}
LAST_STEPS = (0, 3, 5, 4, 6, 1, 0, 1, 5, 3, 6, 2, 5, 4, 2, 6, 0, 0, 5, 4, 6, 3, 3, 6, 5, 6)
F32 = jnp.float32
BF16 = jnp.bfloat16
VMEM_LIMIT = 63 << 20


def dot_nn(a, b):
    return jnp.dot(a, b, preferred_element_type=F32)


def dot_nt(a, b):
    return lax.dot_general(a, b, (((1,), (1,)), ((), ())), preferred_element_type=F32)


def index_bit(index, bit):
    return lax.rem(lax.div(index, 1 << bit), 2)


def flip_bit(index, bit):
    return index + (1 << bit) * (1 - 2 * index_bit(index, bit))


def flip(index, mask):
    for bit in range(mask.bit_length()):
        if (mask >> bit) & 1:
            index = flip_bit(index, bit)
    return index


def halving_plan(rows, cols, bits):
    plan = [("x", rows, cols)]
    for _ in range(bits):
        if rows % 32 == 0:
            rows //= 2
            plan.append(("r", rows, cols))
        elif cols % 256 == 0:
            cols //= 2
            plan.append(("c", rows, cols))
        else:
            plan.append(("x", rows, cols))
    return plan


def step_list(rows, cols, bits, groups, keep, back):
    plan = halving_plan(rows, cols, bits)

    def spans(start, sizes):
        found = []
        for size in [*sizes, *([1] * (bits - start - sum(sizes)))]:
            uncut = any(mode == "x" for mode, _, _ in plan[start + 1 : start + size + 1])
            found += [(start + n, start + n + 1) for n in range(size)] if uncut else [(start, start + size)]
            start += size
        return found

    steps = [(False, *span) for span in spans(0, groups)]
    steps += [(True, *span) for span in reversed(spans(keep, back)) if plan[span[1]][0] != "x"]
    return plan, steps


def peer_masks(bits, groups, keep, back):
    found = set()
    for first, sizes in ((0, groups), (keep, back)):
        for size in [*sizes, *([1] * (len(bits) - first - sum(sizes)))]:
            for choice in range(1, 1 << size):
                mask = [0, 0]
                for number in range(size):
                    if (choice >> number) & 1:
                        axis, bit = bits[first + number]
                        mask[axis] |= 1 << bit
                found.add(tuple(mask))
            first += size
    return found


class Place(typing.NamedTuple):
    seq: jax.Array
    exp: jax.Array
    seq_size: int


def with_rest(bits, seq_size):
    return bits + tuple((0, bit) for bit in range(3, seq_size.bit_length() - 1))


class Reduction:
    def __init__(self, place, buffers, bits, groups, keep, back, on_done):
        self.place, self.bits, self.on_done = place, with_rest(bits, place.seq_size), on_done
        self.array, self.final, self.landing, self.send_sem, self.recv_sem = buffers
        rows, cols = self.array.shape
        self.plan, self.steps = step_list(rows, cols, len(self.bits), groups, keep, back)
        self.mine = [index_bit(place[axis], bit) for axis, bit in self.bits]
        span = (0, rows, 0, cols)
        self.spans = [span]
        for number in range(len(self.bits)):
            span = self.part(span, number, self.mine[number])
            self.spans.append(span)
        self.base = self.spans[keep]
        self.first_sem, total = [], 0
        for _, low, high in self.steps:
            self.first_sem.append(total)
            total += (1 << (high - low)) - 1
        self.position = 0
        self.started = False
        self.done = False

    def part(self, span, number, value):
        mode, rows, cols = self.plan[number + 1]
        row_start, _, col_start, _ = span
        if mode == "r":
            row_start = row_start + value * rows
        elif mode == "c":
            col_start = col_start + value * cols
        return (row_start, rows, col_start, cols)

    def final_view(self, span):
        row_start, rows, col_start, cols = span
        return self.view(
            self.final, (row_start - self.base[0], rows, col_start - self.base[2], cols)
        )

    def view(self, ref, span):
        row_start, rows, col_start, cols = span
        index = []
        for start, size, whole in (
            (row_start, rows, ref.shape[0]),
            (col_start, cols, ref.shape[1]),
        ):
            if size == whole:
                index.append(slice(None))
            else:
                index.append(pl.ds(pl.multiple_of(start, math.gcd(size, 512)), size))
        return ref.at[tuple(index)]

    def copy(self, number, mask):
        gathers, low, high = self.steps[number]
        other = list(self.place[:2])
        span = self.spans[low]
        for bit in range(low, high):
            value = self.mine[bit]
            if (mask >> (bit - low)) & 1:
                axis, index = self.bits[bit]
                other[axis] = flip_bit(other[axis], index)
                value = 1 - value
            span = self.part(span, bit, value)
        if gathers:
            source = target = self.final_view(self.spans[high])
        else:
            source, target = self.view(self.array, span), self.landing[number].at[mask - 1]
        slot = self.first_sem[number] + mask - 1
        return pltpu.make_async_remote_copy(
            src_ref=source,
            dst_ref=target,
            send_sem=self.send_sem.at[slot],
            recv_sem=self.recv_sem.at[slot],
            device_id=tuple(other),
            device_id_type=pl.DeviceIdType.MESH,
        )

    def masks(self, number):
        _, low, high = self.steps[number]
        return range(1, 1 << (high - low))

    def in_place(self, number):
        gathers, _, high = self.steps[number]
        return not gathers and self.plan[high][0] == "x"

    def advance(self):
        if self.done:
            return
        number = self.position
        if self.started:
            gathers, _, high = self.steps[number]
            for mask in self.masks(number):
                self.copy(number, mask).wait_recv()
                if self.in_place(number):
                    self.copy(number, mask).wait_send()
            if not gathers:
                kept = self.view(self.array, self.spans[high])
                total = kept[...].astype(F32)
                for mask in self.masks(number):
                    total += self.landing[number][mask - 1].astype(F32)
                if high == len(self.bits):
                    kept = self.final_view(self.spans[high])
                kept[...] = total.astype(BF16)
            self.position += 1
        number = self.position
        if number < len(self.steps):
            for mask in self.masks(number):
                self.copy(number, mask).start()
            self.started = True
        else:
            for number in range(len(self.steps)):
                if not self.in_place(number):
                    for mask in self.masks(number):
                        self.copy(number, mask).wait_send()
            self.done = True
            self.on_done()


def reduction_buffers(rows, cols, bits, groups, keep, back):
    plan, steps = step_list(rows, cols, bits, groups, keep, back)
    held_rows, held_cols = plan[keep][1:]
    landing = [
        pltpu.VMEM(((1 << (high - low)) - 1, *plan[high][1:]), BF16)
        for gathers, low, high in steps
        if not gathers
    ]
    slots = sum((1 << (high - low)) - 1 for _, low, high in steps)
    sems = pltpu.SemaphoreType.DMA((slots,))
    return [pltpu.VMEM((rows, cols), BF16), pltpu.VMEM((held_rows, held_cols), BF16), landing, sems, sems]


def block_kernel(r, sizes):
    seq_size, exp_size, tokens_own, width, head, top, local_experts, ff, docs = sizes
    all_experts = local_experts * exp_size
    expert_rows = local_experts * head
    flat = all_experts * head
    tile = TILE_TOKENS
    tiles = tokens_own // tile
    cols = top * tile
    chunks = ff // FF_CHUNK
    seq, exp = lax.axis_index("seq"), lax.axis_index("exp")
    place = Place(seq, exp, seq_size)
    near, far = flip_bit(exp, 0), flip_bit(exp, 1)
    across = flip_bit(near, 1)
    near_bit, far_bit = index_bit(exp, 0), index_bit(exp, 1)

    barrier = pltpu.get_barrier_semaphore()
    links = {(0, 1), (0, 2)}
    for sums in (*FFN_SUMS, OUT_SUMS, QUERY_SUMS, SMALL_SUMS):
        links |= peer_masks(with_rest(sums[0], seq_size), *sums[1:])
    partners = [(flip(seq, seq_mask), flip(exp, exp_mask)) for seq_mask, exp_mask in sorted(links)]
    for partner in partners:
        pl.semaphore_signal(
            barrier, inc=1, device_id=partner, device_id_type=pl.DeviceIdType.MESH
        )

    loads = [
        pltpu.make_async_copy(r.w_up, r.up, r.load_sem.at[0]),
        pltpu.make_async_copy(r.w_down, r.down, r.load_sem.at[1]),
        pltpu.make_async_copy(r.cotangent, r.cot, r.load_sem.at[2]),
    ]
    for load in loads:
        load.start()

    inputs = r.tokens[...].astype(F32)
    scale_attn = lax.rsqrt(jnp.mean(inputs * inputs, axis=1, keepdims=True) + NORM_EPSILON)
    r.normed[...] = (inputs * scale_attn * r.gain_attn[...]).astype(BF16)
    r.kv[exp] = dot_nn(r.normed[...], r.w_kv[...]).astype(BF16)
    r.wq[exp] = r.w_query[...]
    r.wo[exp] = r.w_out[...]
    pl.semaphore_wait(barrier, len(partners))

    def gather_copy(kind, step):
        block, target = ((exp, near), (exp, far), (far, near))[step]
        number = kind * 3 + step
        blocks = (r.wq, r.kv, r.wo)[kind]
        return pltpu.make_async_remote_copy(
            src_ref=blocks.at[block],
            dst_ref=blocks.at[block],
            send_sem=r.gather_send.at[number],
            recv_sem=r.gather_recv.at[number],
            device_id=(seq, target),
            device_id_type=pl.DeviceIdType.MESH,
        )

    def gather_start(kind):
        gather_copy(kind, 1).start()
        gather_copy(kind, 0).start()

    def gather_wait(kind, step):
        gather_copy(kind, step).wait_recv()
        if step == 1:
            gather_copy(kind, 2).start()

    gather_start(QUERY)

    def route_row(slot, t):
        return r.routes[slot : slot + 1, t * tile : (t + 1) * tile]

    def gate_row(slot, t):
        return r.gates[slot : slot + 1, t * tile : (t + 1) * tile]

    def add_queries(block, first):
        table = dot_nt(r.wq[block], r.normed[...])
        for t in range(tiles):
            part = table[:, t * tile : (t + 1) * tile]
            for slot in range(top):
                span = slice(slot * tile, (slot + 1) * tile)
                picked = jnp.zeros((head, tile), F32) if first else r.acc[t, :, span]
                for local in range(local_experts):
                    picked = jnp.where(
                        route_row(slot, t) == block * local_experts + local,
                        part[local * head : (local + 1) * head],
                        picked,
                    )
                r.acc[t, :, span] = picked

    add_queries(exp, True)

    ends, total = [], jnp.int32(0)
    for doc in range(docs):
        start, total = total, total + r.lengths[0, doc]
        ends.append((start, total))
    lane = lax.broadcasted_iota(jnp.int32, (tokens_own, 2 * head), 1)
    row = lax.broadcasted_iota(jnp.int32, (tokens_own, 2 * head), 0)

    def prepare_keys(block):
        block_kv = r.kv[block]
        place_of_key = row + block * tokens_own
        extra = jnp.zeros((tokens_own, 2 * head), F32)
        for doc, (start, end) in enumerate(ends):
            outside = (place_of_key < start) | (place_of_key >= end)
            extra = jnp.where((lane == head + doc) & outside, MASKED_SCORE, extra)
        r.kx[block] = jnp.where(lane < head, block_kv.astype(F32), extra).astype(BF16)
        r.kvt[block] = block_kv.T

    prepare_keys(exp)

    gather_wait(QUERY, 1)
    gather_start(KEYS)
    gather_wait(QUERY, 0)
    add_queries(near, False)
    add_queries(far, False)
    gather_wait(QUERY, 2)
    add_queries(across, False)
    extra_row = lax.broadcasted_iota(jnp.int32, (head, cols), 0)
    token_col = lax.rem(lax.broadcasted_iota(jnp.int32, (head, cols), 1), tile)
    for t in range(tiles):
        query = r.acc[t].astype(BF16).astype(F32) * (1.0 / math.sqrt(head))
        place_of_query = token_col + (exp * tokens_own + t * tile)
        inside = jnp.zeros((head, cols), F32)
        for doc, (start, end) in enumerate(ends):
            here = (place_of_query >= start) & (place_of_query < end) & (extra_row == doc)
            inside = jnp.where(here, 1.0, inside)
        r.qt[t, :head] = query.astype(BF16)
        r.qt[t, head:] = inside.astype(BF16)

    key_in_tile = lax.broadcasted_iota(jnp.int32, (tile, cols), 0)
    token_in_tile = lax.rem(lax.broadcasted_iota(jnp.int32, (tile, cols), 1), tile)
    for t in range(tiles):
        edge = t * tile
        query = r.qt[t]
        last = jnp.where(
            key_in_tile <= token_in_tile,
            dot_nn(r.kx[exp, edge : edge + tile], query),
            MASKED_SCORE,
        )
        top_score = jnp.max(last, axis=0, keepdims=True)
        if t > 0:
            early = dot_nn(r.kx[exp, :edge], query)
            top_score = jnp.maximum(top_score, jnp.max(early, axis=0, keepdims=True))
        weight = jnp.exp(last - top_score)
        total_weight = jnp.sum(weight, axis=0, keepdims=True)
        summed = dot_nn(r.kvt[exp, head:, edge : edge + tile], weight.astype(BF16))
        if t > 0:
            weight = jnp.exp(early - top_score)
            total_weight += jnp.sum(weight, axis=0, keepdims=True)
            summed += dot_nn(r.kvt[exp, head:, :edge], weight.astype(BF16))
        r.peak[t], r.total[t], r.acc[t] = top_score, total_weight, summed

    def forward_block(block):
        prepare_keys(block)

        def forward_tile(t, carry):
            scores = dot_nn(r.kx[block], r.qt[t])
            old = r.peak[t]
            new = jnp.maximum(old, jnp.max(scores, axis=0, keepdims=True))
            weight = jnp.exp(scores - new)
            fade = jnp.exp(old - new)
            r.peak[t] = new
            r.total[t] = r.total[t] * fade + jnp.sum(weight, axis=0, keepdims=True)
            r.acc[t] = r.acc[t] * fade + dot_nn(r.kvt[block, head:], weight.astype(BF16))
            return carry

        lax.fori_loop(0, tiles, forward_tile, 0)

    gather_wait(KEYS, 0)
    pl.when(near < exp)(lambda: forward_block(near))
    gather_wait(KEYS, 1)
    gather_start(OUT)
    pl.when(far < exp)(lambda: forward_block(far))
    gather_wait(KEYS, 2)
    pl.when(across < exp)(lambda: forward_block(across))
    for t in range(tiles):
        r.acc[t] = (r.acc[t] / r.total[t]).astype(BF16).astype(F32)
        r.peak[t] = r.peak[t] + jnp.log(r.total[t])

    for t in range(tiles):
        shares = [
            r.acc[t, :, slot * tile : (slot + 1) * tile] * gate_row(slot, t)
            for slot in range(top)
        ]
        for expert in range(all_experts):
            spread = jnp.zeros((head, tile), F32)
            for slot in range(top):
                spread = jnp.where(route_row(slot, t) == expert, shares[slot], spread)
            r.spread[expert * head : (expert + 1) * head, t * tile : (t + 1) * tile] = (
                spread.astype(BF16)
            )
    gather_wait(OUT, 1)
    gather_wait(OUT, 0)
    gather_wait(OUT, 2)
    r.wo_flat[...] = r.wo[...].reshape(flat, width)
    r.mixed[...] = r.tokens[...].astype(F32) + dot_nn(r.spread[...].T, r.wo_flat[...])

    mixed = r.mixed[...]
    scale_ffn = lax.rsqrt(jnp.mean(mixed * mixed, axis=1, keepdims=True) + NORM_EPSILON)
    r.nf[...] = (mixed * scale_ffn * r.gain_ffn[...]).astype(BF16)
    r.nft[...] = r.nf[...].T
    for load in loads:
        load.wait()

    stores = []

    def store(source, target):
        def begin():
            copy = pltpu.make_async_copy(source, target, r.store_sem.at[len(stores)])
            stores.append((source, target, len(stores)))
            copy.start()

        return begin

    def store_chunk(chunk):
        span = slice(chunk * FF_CHUNK, (chunk + 1) * FF_CHUNK)
        array = r.ffn[chunk][1]
        first = store(array.at[:FF_CHUNK], r.grad_down.at[span])
        second = store(array.at[FF_CHUNK:], r.grad_up.at[:, span])

        def begin():
            first()
            second()

        return begin

    ffn = [
        Reduction(place, r.ffn[chunk], *FFN_SUMS[chunk], store_chunk(chunk))
        for chunk in range(chunks)
    ]
    red_out = Reduction(place, r.out_sums, *OUT_SUMS, store(r.out_sums[1], r.grad_out))
    red_query = Reduction(place, r.query_sums, *QUERY_SUMS, store(r.query_sums[1], r.grad_query))
    red_small = Reduction(place, r.small_sums, *SMALL_SUMS, store(r.small_sums[1], r.grad_small))

    def store_by_owner(target, table):
        for block in range(exp_size):
            spot = (block % 2) * 2 + block // 2
            target[spot * expert_rows : (spot + 1) * expert_rows] = table[
                block * expert_rows : (block + 1) * expert_rows
            ].astype(BF16)

    moving = [*ffn, red_out, red_query, red_small]

    def hook(point):
        for one in SCHEDULE.get(point, ()):
            moving[one].advance()

    root = math.sqrt(2.0 / math.pi)
    for chunk in range(chunks):
        span = slice(chunk * FF_CHUNK, (chunk + 1) * FF_CHUNK)
        hidden = dot_nn(r.nf[...], r.up[:, span])
        grad_active = dot_nt(r.cot[...], r.down[span])
        square = hidden * hidden
        bent = jnp.tanh(root * hidden * (1.0 + 0.044715 * square))
        half = 0.5 * (1.0 + bent)
        active = (hidden * half).astype(BF16)
        slope = half + 0.5 * hidden * (1.0 - bent * bent) * (
            root * (1.0 + 3 * 0.044715 * square)
        )
        grad_hidden = (grad_active * slope).astype(BF16)
        r.ffn[chunk][0][:FF_CHUNK] = dot_nn(active.T, r.cot[...]).astype(BF16)
        r.ffn[chunk][0][FF_CHUNK:] = dot_nn(r.nft[...], grad_hidden).astype(BF16)
        ffn[chunk].advance()
        hook((0, 2 * chunk))
        out_part = dot_nn(active, r.down[span])
        grad_part = dot_nt(grad_hidden, r.up[:, span])
        if chunk == 0:
            r.sum_out[...], r.sum_grad[...] = out_part, grad_part
        else:
            r.sum_out[...] += out_part
            r.sum_grad[...] += grad_part
        hook((0, 2 * chunk + 1))

    mixed = r.mixed[...]
    r.block_out[...] = (mixed + r.sum_out[...]).astype(BF16)
    grad_nf = r.sum_grad[...]
    scale_ffn = lax.rsqrt(jnp.mean(mixed * mixed, axis=1, keepdims=True) + NORM_EPSILON)
    gained = grad_nf * r.gain_ffn[...]
    inner = jnp.mean(gained * mixed, axis=1, keepdims=True)
    grad_gain_ffn = jnp.sum(grad_nf * mixed * scale_ffn, axis=0, keepdims=True)
    grad_mixed = (
        r.cot[...].astype(F32)
        + scale_ffn * gained
        - mixed * (scale_ffn * scale_ffn * scale_ffn * inner)
    )
    r.grad_mixed[...] = grad_mixed
    r.gm[...] = grad_mixed.astype(BF16)
    store_by_owner(r.out_sums[0], dot_nn(r.spread[...], r.gm[...]))
    red_out.advance()
    hook((1, 0))

    table = dot_nt(r.wo_flat[...], r.gm[...])
    for t in range(tiles):
        for slot in range(top):
            span = slice(slot * tile, (slot + 1) * tile)
            picked = jnp.zeros((head, tile), F32)
            for expert in range(all_experts):
                picked = jnp.where(
                    route_row(slot, t) == expert,
                    table[expert * head : (expert + 1) * head, t * tile : (t + 1) * tile],
                    picked,
                )
            grad = (picked * gate_row(slot, t)).astype(BF16)
            r.dot[t, head:, span] = grad
            r.dot[t, :head, span] = jnp.zeros((head, tile), BF16)
            r.delta[t, :, span] = jnp.sum(
                grad.astype(F32) * r.acc[t, :, span], axis=0, keepdims=True
            )
        both = jnp.concatenate([r.qt[t, :head], r.dot[t, head:]], axis=0).T
        left = lax.broadcasted_iota(jnp.int32, (cols, 2 * head), 1) < head
        r.rows[t, :cols] = jnp.where(left, both, jnp.zeros((), BF16))
        r.rows[t, cols:] = jnp.where(left, jnp.zeros((), BF16), both)
        r.acc[t] = jnp.zeros((head, cols), F32)
    hook((1, 1))

    def backward_piece(t, scores, key_values, keys_t):
        weight = jnp.exp(scores - r.peak[t])
        grad_weight = dot_nn(key_values, r.dot[t])
        grad_scores = (weight * (grad_weight - r.delta[t])).astype(BF16)
        r.acc[t] += dot_nn(keys_t, grad_scores)
        return dot_nn(grad_scores, r.rows[t, :cols]) + dot_nn(
            weight.astype(BF16), r.rows[t, cols:]
        )

    def kv_copy(step):
        target = (near, far, near)[step]
        return pltpu.make_async_remote_copy(
            src_ref=r.gkv_out.at[step],
            dst_ref=r.gkv_in.at[step],
            send_sem=r.gkv_send.at[step],
            recv_sem=r.gkv_recv.at[step],
            device_id=(seq, target),
            device_id_type=pl.DeviceIdType.MESH,
        )

    def send_across():
        r.gkv_out[0] = r.gkv[...].astype(BF16)
        kv_copy(0).start()

    def send_far():
        kv_copy(0).wait_recv()
        r.gkv_out[1] = (r.gkv[...] + r.gkv_in[0].astype(F32)).astype(BF16)
        kv_copy(1).start()

    def send_near():
        r.gkv_out[2] = r.gkv[...].astype(BF16)
        kv_copy(2).start()

    def backward_step(step, carry):
        turn, t = lax.div(step, tiles), lax.rem(step, tiles)
        block = jnp.where(turn == 0, across, jnp.where(turn == 1, far, near))

        @pl.when(t == 0)
        def _():
            r.gkv[...] = jnp.zeros((tokens_own, 2 * head), F32)

        @pl.when(block < exp)
        def _():
            scores = dot_nn(r.kx[block], r.qt[t])
            piece = backward_piece(t, scores, r.kv[block], r.kvt[block, :head])

            r.gkv[...] += piece

        pl.when((step == tiles - 1) & (far_bit == 1))(send_across)
        pl.when((step == 2 * tiles - 1) & (far_bit == 1))(send_far)
        pl.when((step == 3 * tiles - 1) & (near_bit == 1))(send_near)
        for turn_step in range(3 * tiles):
            if (2, turn_step) in SCHEDULE:
                pl.when(step == turn_step)(functools.partial(hook, (2, turn_step)))
        return carry

    lax.fori_loop(0, 3 * tiles, backward_step, 0)

    r.gkv[...] = jnp.zeros((tokens_own, 2 * head), F32)
    for t in range(tiles):
        edge = t * tile
        scores = jnp.where(
            key_in_tile <= token_in_tile,
            dot_nn(r.kx[exp, edge : edge + tile], r.qt[t]),
            MASKED_SCORE,
        )
        r.gkv[edge : edge + tile] += backward_piece(
            t, scores, r.kv[exp, edge : edge + tile], r.kvt[exp, :head, edge : edge + tile]
        )
        if t > 0:
            scores = dot_nn(r.kx[exp, :edge], r.qt[t])
            r.gkv[:edge] += backward_piece(
                t, scores, r.kv[exp, :edge], r.kvt[exp, :head, :edge]
            )
        hook((3, t))

    for t in range(tiles):
        shares = [
            (r.acc[t, :, slot * tile : (slot + 1) * tile] * (1.0 / math.sqrt(head)))
            .astype(BF16)
            .astype(F32)
            for slot in range(top)
        ]
        for expert in range(all_experts):
            spread = jnp.zeros((head, tile), F32)
            for slot in range(top):
                spread = jnp.where(route_row(slot, t) == expert, shares[slot], spread)
            r.spread[expert * head : (expert + 1) * head, t * tile : (t + 1) * tile] = (
                spread.astype(BF16)
            )
    store_by_owner(r.query_sums[0], dot_nn(r.spread[...], r.normed[...]))
    red_query.advance()

    @pl.when(near_bit == 0)
    def _():
        kv_copy(2).wait_recv()
        r.gkv[...] += r.gkv_in[2].astype(F32)

    @pl.when(far_bit == 0)
    def _():
        kv_copy(1).wait_recv()
        r.gkv[...] += r.gkv_in[1].astype(F32)

    grad_kv = r.gkv[...].astype(BF16)
    wq_flat = r.wq[...].reshape(flat, width)
    grad_normed = dot_nn(r.spread[...].T, wq_flat) + dot_nt(grad_kv, r.w_kv[...])
    inputs = r.tokens[...].astype(F32)
    scale_attn = lax.rsqrt(jnp.mean(inputs * inputs, axis=1, keepdims=True) + NORM_EPSILON)
    grad_gain_attn = jnp.sum(grad_normed * inputs * scale_attn, axis=0, keepdims=True)
    r.small_sums[0][: 2 * head] = dot_nn(grad_kv.T, r.normed[...]).astype(BF16)
    gain_rows = r.small_sums[0].shape[0] - 2 * head
    which = lax.broadcasted_iota(jnp.int32, (gain_rows, width), 0)
    r.small_sums[0][2 * head :] = jnp.where(
        which == 0, grad_gain_attn, jnp.where(which == 1, grad_gain_ffn, 0.0)
    ).astype(BF16)
    red_small.advance()
    gained = grad_normed * r.gain_attn[...]
    inner = jnp.mean(gained * inputs, axis=1, keepdims=True)
    r.grad_tokens[...] = (
        r.grad_mixed[...]
        + scale_attn * gained
        - inputs * (scale_attn * scale_attn * scale_attn * inner)
    ).astype(BF16)

    for one in LAST_STEPS:
        moving[one].advance()
    while not all(one.done for one in moving):
        for one in moving:
            one.advance()
    for kind in (QUERY, KEYS, OUT):
        for step in range(3):
            gather_copy(kind, step).wait_send()

    @pl.when(far_bit == 1)
    def _():
        kv_copy(0).wait_send()
        kv_copy(1).wait_send()

    pl.when(near_bit == 1)(lambda: kv_copy(2).wait_send())
    for source, target, number in stores:
        pltpu.make_async_copy(source, target, r.store_sem.at[number]).wait()


def finish_kernel(
    block_out, grad_tokens, grad_up, grad_down, grad_query, grad_out, small, *results
):
    out, tokens, gain_attn, kv, query, projection, gain_ffn, up, down = results
    out[...] = block_out[...]
    tokens[...] = grad_tokens[...]
    up[...] = grad_up[...].astype(F32)
    down[...] = grad_down[...].astype(F32)

    @pl.when(pl.program_id(0) == 0)
    def _():
        experts, head, _ = projection.shape
        sums = small[...].astype(F32)
        kv[...] = sums[: 2 * head].T
        gain_attn[...] = sums[2 * head : 2 * head + 1]
        gain_ffn[...] = sums[2 * head + 1 : 2 * head + 2]
        for expert in range(experts):
            rows = slice(expert * head, (expert + 1) * head)
            query[expert] = grad_query[rows].astype(F32).T
            projection[expert] = grad_out[rows].astype(F32)


def per_device(
    seq_size,
    exp_size,
    tokens,
    lengths,
    routes,
    gates,
    gain_attn,
    w_kv,
    w_query,
    w_out,
    gain_ffn,
    w_up,
    w_down,
    cotangent,
):
    tokens_own, width = tokens.shape
    top = routes.shape[1]
    local_experts, _, head = w_query.shape
    ff = w_up.shape[1]
    docs = lengths.shape[1]
    tiles = tokens_own // TILE_TOKENS
    cols = top * TILE_TOKENS
    chunks = ff // FF_CHUNK
    expert_rows = local_experts * head
    flat = expert_rows * exp_size
    stages = seq_size.bit_length() - 1 + exp_size.bit_length() - 1
    small_rows = 4 * head
    sizes = (seq_size, exp_size, tokens_own, width, head, top, local_experts, ff, docs)

    vmem = pl.BlockSpec(memory_space=pltpu.VMEM)
    smem = pl.BlockSpec(memory_space=pltpu.SMEM)
    anywhere = pl.BlockSpec(memory_space=pl.ANY)
    inputs = dict(
        lengths=(lengths, smem),
        tokens=(tokens, vmem),
        routes=(routes.T, vmem),
        gates=(gates.T, vmem),
        gain_attn=(gain_attn.reshape(1, width), vmem),
        w_kv=(w_kv, vmem),
        w_query=(jnp.swapaxes(w_query, 1, 2).reshape(expert_rows, width), vmem),
        w_out=(w_out.reshape(expert_rows, width), vmem),
        gain_ffn=(gain_ffn.reshape(1, width), vmem),
        w_up=(w_up, anywhere),
        w_down=(w_down, anywhere),
        cotangent=(cotangent, anywhere),
    )
    outputs = dict(
        block_out=((tokens_own, width), vmem),
        grad_tokens=((tokens_own, width), vmem),
        grad_up=((width, ff), anywhere),
        grad_down=((ff, width), anywhere),
        grad_query=((expert_rows, width), anywhere),
        grad_out=((expert_rows, width), anywhere),
        grad_small=((small_rows, width), anywhere),
    )
    scratch = dict(
        up=pltpu.VMEM((width, ff), BF16),
        down=pltpu.VMEM((ff, width), BF16),
        cot=pltpu.VMEM((tokens_own, width), BF16),
        normed=pltpu.VMEM((tokens_own, width), BF16),
        wq=pltpu.VMEM((exp_size, expert_rows, width), BF16),
        wo=pltpu.VMEM((exp_size, expert_rows, width), BF16),
        wo_flat=pltpu.VMEM((flat, width), BF16),
        kv=pltpu.VMEM((exp_size, tokens_own, 2 * head), BF16),
        kx=pltpu.VMEM((exp_size, tokens_own, 2 * head), BF16),
        kvt=pltpu.VMEM((exp_size, 2 * head, tokens_own), BF16),
        qt=pltpu.VMEM((tiles, 2 * head, cols), BF16),
        dot=pltpu.VMEM((tiles, 2 * head, cols), BF16),
        rows=pltpu.VMEM((tiles, 2 * cols, 2 * head), BF16),
        acc=pltpu.VMEM((tiles, head, cols), F32),
        peak=pltpu.VMEM((tiles, 1, cols), F32),
        total=pltpu.VMEM((tiles, 1, cols), F32),
        delta=pltpu.VMEM((tiles, 1, cols), F32),
        spread=pltpu.VMEM((flat, tokens_own), BF16),
        mixed=pltpu.VMEM((tokens_own, width), F32),
        nf=pltpu.VMEM((tokens_own, width), BF16),
        nft=pltpu.VMEM((width, tokens_own), BF16),
        sum_out=pltpu.VMEM((tokens_own, width), F32),
        sum_grad=pltpu.VMEM((tokens_own, width), F32),
        grad_mixed=pltpu.VMEM((tokens_own, width), F32),
        gm=pltpu.VMEM((tokens_own, width), BF16),
        gkv=pltpu.VMEM((tokens_own, 2 * head), F32),
        gkv_out=pltpu.VMEM((3, tokens_own, 2 * head), BF16),
        gkv_in=pltpu.VMEM((3, tokens_own, 2 * head), BF16),
        load_sem=pltpu.SemaphoreType.DMA((3,)),
        store_sem=pltpu.SemaphoreType.DMA((2 * chunks + 3,)),
        gather_send=pltpu.SemaphoreType.DMA((9,)),
        gather_recv=pltpu.SemaphoreType.DMA((9,)),
        gkv_send=pltpu.SemaphoreType.DMA((3,)),
        gkv_recv=pltpu.SemaphoreType.DMA((3,)),
    )

    def buffers(rows, sums):
        return reduction_buffers(rows, width, stages, *sums[1:])

    scratch.update(
        ffn=[buffers(width + FF_CHUNK, FFN_SUMS[chunk]) for chunk in range(chunks)],
        out_sums=buffers(flat, OUT_SUMS),
        query_sums=buffers(flat, QUERY_SUMS),
        small_sums=buffers(small_rows, SMALL_SUMS),
    )
    scratch_list, scratch_tree = jax.tree.flatten(scratch)

    def kernel(*refs):
        names = [*inputs, *outputs]
        held = jax.tree.unflatten(scratch_tree, refs[len(names) :])
        block_kernel(types.SimpleNamespace(**dict(zip(names, refs)), **held), sizes)

    block_out, grad_tokens, grad_up, grad_down, grad_query, grad_out, small = pl.pallas_call(
        kernel,
        out_shape=[jax.ShapeDtypeStruct(shape, BF16) for shape, _ in outputs.values()],
        in_specs=[spec for _, spec in inputs.values()],
        out_specs=[spec for _, spec in outputs.values()],
        scratch_shapes=scratch_list,
        compiler_params=pltpu.CompilerParams(
            collective_id=0, has_side_effects=True, vmem_limit_bytes=VMEM_LIMIT
        ),
    )(*[array for array, _ in inputs.values()])
    split = FINISH_STEPS
    whole = lambda shape: pl.BlockSpec(shape, lambda step: (0,) * len(shape))
    rows_of = lambda rows, cols: pl.BlockSpec((rows // split, cols), lambda step: (step, 0))
    shapes = (
        ((tokens_own, width), BF16),
        ((tokens_own, width), BF16),
        ((1, width), F32),
        ((width, 2 * head), F32),
        ((local_experts, width, head), F32),
        ((local_experts, head, width), F32),
        ((1, width), F32),
        ((width, ff), F32),
        ((ff, width), F32),
    )
    by_token, by_width, by_unit = rows_of(tokens_own, width), rows_of(width, ff), rows_of(ff, width)
    results = pl.pallas_call(
        finish_kernel,
        grid=(split,),
        out_shape=[jax.ShapeDtypeStruct(*shape) for shape in shapes],
        in_specs=[by_token, by_token, by_width, by_unit]
        + [whole(array.shape) for array in (grad_query, grad_out, small)],
        out_specs=[by_token, by_token]
        + [whole(shape) for shape, _ in shapes[2:7]]
        + [by_width, by_unit],
    )(block_out, grad_tokens, grad_up, grad_down, grad_query, grad_out, small)
    return tuple(
        result.reshape(width) if result.shape == (1, width) else result for result in results
    )


def solution(mesh):
    sizes = dict(mesh.shape)
    return jax.shard_map(
        functools.partial(per_device, sizes["seq"], sizes["exp"]),
        mesh=mesh,
        in_specs=(
            P(("seq", "exp"), None),
            P("seq", None),
            P(("seq", "exp"), None),
            P(("seq", "exp"), None),
            P(),
            P(),
            P("exp", None, None),
            P("exp", None, None),
            P(),
            P(),
            P(),
            P(("seq", "exp"), None),
        ),
        out_specs=(
            P(("seq", "exp"), None),
            P(("seq", "exp"), None),
            P(),
            P(),
            P("exp", None, None),
            P("exp", None, None),
            P(),
            P(),
            P(),
        ),
        check_vma=False,
    )
```

```python
import functools
import math
import types
import typing

import jax
import jax.numpy as jnp
from jax import lax
from jax.experimental import pallas as pl
from jax.experimental.pallas import tpu as pltpu
from jax.sharding import PartitionSpec as P

NORM_EPSILON = 1e-06
MASKED_SCORE = -1e30
TILE_TOKENS = 256
QUERY, KEYS, OUT = range(3)
FF_CHUNK = 512
FINISH_PIECES = 4
FINISH_VMEM = 62 << 20
CORE, Y, X, Z0, Z1 = ((1, 0), (1, 1), (0, 0), (0, 1), (0, 2))
FFN_SUMS = (
    ((CORE, Y, X, Z0, Z1), (1, 2, 1, 1), 0, (1, 1, 1, 1, 1)),
    ((CORE, Z0, Z1, X, Y), (1, 2, 2), 0, (1, 2, 2)),
    ((CORE, X, Y, Z0, Z1), (1, 2, 2), 0, (1, 2, 2)),
    ((CORE, Y, X, Z0, Z1), (1, 2, 2), 0, (1, 1, 1, 2)),
)
OUT_SUMS = ((CORE, Y, X, Z0, Z1), (1, 2, 2), 2, (1, 1, 1))
QUERY_SUMS = ((CORE, Y, X, Z0, Z1), (1, 1, 1, 2), 2, (3,))
SMALL_SUMS = ((CORE, Y, X, Z0, Z1), (1, 1, 3), 0, (1, 1, 3))
SCHEDULE = {
    (0, 4): (0,),
    (0, 6): (1,),
    (1, 0): (2, 3),
    (2, 0): (4,),
    (2, 1): (0,),
    (2, 3): (2,),
    (2, 4): (0, 1),
    (2, 5): (3,),
    (2, 6): (2,),
    (2, 7): (0, 4, 1),
    (2, 8): (3,),
    (3, 1): (2,),
    (3, 2): (0, 1),
}
LAST_STEPS = (4, 5, 3, 6, 0, 7, 2, 2, 5, 3, 6, 7, 0, 5, 1, 6, 4, 1, 7, 5, 3, 6, 4, 3, 7, 0, 5, 4, 7, 0, 6, 7)
F32 = jnp.float32
BF16 = jnp.bfloat16
VMEM_LIMIT = 63 << 20


def dot_nn(a, b):
    return jnp.dot(a, b, preferred_element_type=F32)


def dot_nt(a, b):
    return lax.dot_general(a, b, (((1,), (1,)), ((), ())), preferred_element_type=F32)


def index_bit(index, bit):
    return lax.rem(lax.div(index, 1 << bit), 2)


def flip_bit(index, bit):
    return index + (1 << bit) * (1 - 2 * index_bit(index, bit))


def flip(index, mask):
    for bit in range(mask.bit_length()):
        if (mask >> bit) & 1:
            index = flip_bit(index, bit)
    return index


def halving_plan(rows, cols, bits):
    plan = [("x", rows, cols)]
    for _ in range(bits):
        if rows % 32 == 0:
            rows //= 2
            plan.append(("r", rows, cols))
        elif cols % 256 == 0:
            cols //= 2
            plan.append(("c", rows, cols))
        else:
            plan.append(("x", rows, cols))
    return plan


def step_list(rows, cols, bits, groups, keep, back):
    plan = halving_plan(rows, cols, bits)

    def spans(start, sizes):
        found = []
        for size in [*sizes, *([1] * (bits - start - sum(sizes)))]:
            uncut = any(mode == "x" for mode, _, _ in plan[start + 1 : start + size + 1])
            found += [(start + n, start + n + 1) for n in range(size)] if uncut else [(start, start + size)]
            start += size
        return found

    steps = [(False, *span) for span in spans(0, groups)]
    steps += [(True, *span) for span in reversed(spans(keep, back)) if plan[span[1]][0] != "x"]
    return plan, steps


def peer_masks(bits, groups, keep, back):
    found = set()
    for first, sizes in ((0, groups), (keep, back)):
        for size in [*sizes, *([1] * (len(bits) - first - sum(sizes)))]:
            for choice in range(1, 1 << size):
                mask = [0, 0]
                for number in range(size):
                    if (choice >> number) & 1:
                        axis, bit = bits[first + number]
                        mask[axis] |= 1 << bit
                found.add(tuple(mask))
            first += size
    return found


class Place(typing.NamedTuple):
    seq: jax.Array
    exp: jax.Array
    seq_size: int


def with_rest(bits, seq_size):
    return bits + tuple((0, bit) for bit in range(3, seq_size.bit_length() - 1))


class Reduction:
    def __init__(self, place, buffers, bits, groups, keep, back, on_done):
        self.place, self.bits, self.on_done = place, with_rest(bits, place.seq_size), on_done
        self.array, self.final, self.landing, self.send_sem, self.recv_sem = buffers
        rows, cols = self.array.shape
        self.plan, self.steps = step_list(rows, cols, len(self.bits), groups, keep, back)
        self.mine = [index_bit(place[axis], bit) for axis, bit in self.bits]
        span = (0, rows, 0, cols)
        self.spans = [span]
        for number in range(len(self.bits)):
            span = self.part(span, number, self.mine[number])
            self.spans.append(span)
        self.base = self.spans[keep]
        self.first_sem, total = [], 0
        for _, low, high in self.steps:
            self.first_sem.append(total)
            total += (1 << (high - low)) - 1
        self.position = 0
        self.started = False
        self.done = False

    def part(self, span, number, value):
        mode, rows, cols = self.plan[number + 1]
        row_start, _, col_start, _ = span
        if mode == "r":
            row_start = row_start + value * rows
        elif mode == "c":
            col_start = col_start + value * cols
        return (row_start, rows, col_start, cols)

    def final_view(self, span):
        row_start, rows, col_start, cols = span
        return self.view(
            self.final, (row_start - self.base[0], rows, col_start - self.base[2], cols)
        )

    def view(self, ref, span):
        row_start, rows, col_start, cols = span
        index = []
        for start, size, whole in (
            (row_start, rows, ref.shape[0]),
            (col_start, cols, ref.shape[1]),
        ):
            if size == whole:
                index.append(slice(None))
            else:
                index.append(pl.ds(pl.multiple_of(start, math.gcd(size, 512)), size))
        return ref.at[tuple(index)]

    def copy(self, number, mask):
        gathers, low, high = self.steps[number]
        other = list(self.place[:2])
        span = self.spans[low]
        for bit in range(low, high):
            value = self.mine[bit]
            if (mask >> (bit - low)) & 1:
                axis, index = self.bits[bit]
                other[axis] = flip_bit(other[axis], index)
                value = 1 - value
            span = self.part(span, bit, value)
        if gathers:
            source = target = self.final_view(self.spans[high])
        else:
            source, target = self.view(self.array, span), self.landing[number].at[mask - 1]
        slot = self.first_sem[number] + mask - 1
        return pltpu.make_async_remote_copy(
            src_ref=source,
            dst_ref=target,
            send_sem=self.send_sem.at[slot],
            recv_sem=self.recv_sem.at[slot],
            device_id=tuple(other),
            device_id_type=pl.DeviceIdType.MESH,
        )

    def masks(self, number):
        _, low, high = self.steps[number]
        return range(1, 1 << (high - low))

    def in_place(self, number):
        gathers, _, high = self.steps[number]
        return not gathers and self.plan[high][0] == "x"

    def advance(self):
        if self.done:
            return
        number = self.position
        if self.started:
            gathers, _, high = self.steps[number]
            for mask in self.masks(number):
                self.copy(number, mask).wait_recv()
                if self.in_place(number):
                    self.copy(number, mask).wait_send()
            if not gathers:
                kept = self.view(self.array, self.spans[high])
                total = kept[...].astype(F32)
                for mask in self.masks(number):
                    total += self.landing[number][mask - 1].astype(F32)
                if high == len(self.bits):
                    kept = self.final_view(self.spans[high])
                kept[...] = total.astype(BF16)
            self.position += 1
        number = self.position
        if number < len(self.steps):
            for mask in self.masks(number):
                self.copy(number, mask).start()
            self.started = True
        else:
            for number in range(len(self.steps)):
                if not self.in_place(number):
                    for mask in self.masks(number):
                        self.copy(number, mask).wait_send()
            self.done = True
            self.on_done()


def reduction_buffers(rows, cols, bits, groups, keep, back):
    plan, steps = step_list(rows, cols, bits, groups, keep, back)
    held_rows, held_cols = plan[keep][1:]
    landing = [
        pltpu.VMEM(((1 << (high - low)) - 1, *plan[high][1:]), BF16)
        for gathers, low, high in steps
        if not gathers
    ]
    slots = sum((1 << (high - low)) - 1 for _, low, high in steps)
    sems = pltpu.SemaphoreType.DMA((slots,))
    return [pltpu.VMEM((rows, cols), BF16), pltpu.VMEM((held_rows, held_cols), BF16), landing, sems, sems]


def block_kernel(r, sizes):
    seq_size, exp_size, tokens_own, width, head, top, local_experts, ff, docs = sizes
    all_experts = local_experts * exp_size
    expert_rows = local_experts * head
    flat = all_experts * head
    tile = TILE_TOKENS
    tiles = tokens_own // tile
    cols = top * tile
    chunks = ff // FF_CHUNK
    seq, exp = lax.axis_index("seq"), lax.axis_index("exp")
    place = Place(seq, exp, seq_size)
    near, far = flip_bit(exp, 0), flip_bit(exp, 1)
    across = flip_bit(near, 1)
    near_bit, far_bit = index_bit(exp, 0), index_bit(exp, 1)

    barrier = pltpu.get_barrier_semaphore()
    links = {(0, 1), (0, 2)}
    for sums in (*FFN_SUMS, OUT_SUMS, QUERY_SUMS, SMALL_SUMS):
        links |= peer_masks(with_rest(sums[0], seq_size), *sums[1:])
    partners = [(flip(seq, seq_mask), flip(exp, exp_mask)) for seq_mask, exp_mask in sorted(links)]
    for partner in partners:
        pl.semaphore_signal(
            barrier, inc=1, device_id=partner, device_id_type=pl.DeviceIdType.MESH
        )

    arrays = (
        (r.tokens, r.tok),
        (r.w_query, r.wq.at[exp]),
        (r.w_out, r.wo.at[exp]),
        (r.cotangent, r.cot),
        (r.w_down, r.down),
        (r.w_up, r.up),
    )
    loads = [
        pltpu.make_async_copy(source, target, r.load_sem.at[number])
        for number, (source, target) in enumerate(arrays)
    ]
    for load in loads:
        load.start()
    loads[0].wait()

    inputs = r.tok[...].astype(F32)
    scale_attn = lax.rsqrt(jnp.mean(inputs * inputs, axis=1, keepdims=True) + NORM_EPSILON)
    r.normed[...] = (inputs * scale_attn * r.gain_attn[...]).astype(BF16)
    r.kv[exp] = dot_nn(r.normed[...], r.w_kv[...]).astype(BF16)
    pl.semaphore_wait(barrier, len(partners))

    def gather_copy(kind, step):
        block, target = ((exp, near), (exp, far), (far, near))[step]
        number = kind * 3 + step
        blocks = (r.wq, r.kv, r.wo)[kind]
        own = (r.w_query, r.kv.at[exp], r.w_out)[kind]
        return pltpu.make_async_remote_copy(
            src_ref=own if step < 2 else blocks.at[block],
            dst_ref=blocks.at[block],
            send_sem=r.gather_send.at[number],
            recv_sem=r.gather_recv.at[number],
            device_id=(seq, target),
            device_id_type=pl.DeviceIdType.MESH,
        )

    def gather_start(kind):
        gather_copy(kind, 1).start()
        gather_copy(kind, 0).start()

    def gather_wait(kind, step):
        gather_copy(kind, step).wait_recv()
        if step == 1:
            gather_copy(kind, 2).start()

    gather_start(QUERY)

    def route_row(slot, t):
        return r.routes[slot : slot + 1, t * tile : (t + 1) * tile]

    def gate_row(slot, t):
        return r.gates[slot : slot + 1, t * tile : (t + 1) * tile]

    def add_queries(block, first):
        table = dot_nt(r.wq[block], r.normed[...])
        for t in range(tiles):
            part = table[:, t * tile : (t + 1) * tile]
            for slot in range(top):
                span = slice(slot * tile, (slot + 1) * tile)
                picked = jnp.zeros((head, tile), F32) if first else r.acc[t, :, span]
                for local in range(local_experts):
                    picked = jnp.where(
                        route_row(slot, t) == block * local_experts + local,
                        part[local * head : (local + 1) * head],
                        picked,
                    )
                r.acc[t, :, span] = picked

    loads[1].wait()
    add_queries(exp, True)

    ends, total = [], jnp.int32(0)
    for doc in range(docs):
        start, total = total, total + r.lengths[0, doc]
        ends.append((start, total))
    lane = lax.broadcasted_iota(jnp.int32, (tokens_own, 2 * head), 1)
    row = lax.broadcasted_iota(jnp.int32, (tokens_own, 2 * head), 0)

    def prepare_keys(block):
        block_kv = r.kv[block]
        place_of_key = row + block * tokens_own
        extra = jnp.zeros((tokens_own, 2 * head), F32)
        for doc, (start, end) in enumerate(ends):
            outside = (place_of_key < start) | (place_of_key >= end)
            extra = jnp.where((lane == head + doc) & outside, MASKED_SCORE, extra)
        r.kx[block] = jnp.where(lane < head, block_kv.astype(F32), extra).astype(BF16)
        r.kvt[block] = block_kv.T

    prepare_keys(exp)

    gather_wait(QUERY, 0)
    add_queries(near, False)

    loads[3].wait()
    loads[4].wait()
    for chunk in range(chunks):
        span = slice(chunk * FF_CHUNK, (chunk + 1) * FF_CHUNK)
        r.grad_hidden[:, span] = dot_nt(r.cot[...], r.down[span]).astype(BF16)
    gather_copy(QUERY, 1).wait_send()
    gather_start(KEYS)
    gather_wait(QUERY, 1)
    add_queries(far, False)
    gather_wait(QUERY, 2)
    add_queries(across, False)
    extra_row = lax.broadcasted_iota(jnp.int32, (head, cols), 0)
    token_col = lax.rem(lax.broadcasted_iota(jnp.int32, (head, cols), 1), tile)
    for t in range(tiles):
        query = r.acc[t].astype(BF16).astype(F32) * (1.0 / math.sqrt(head))
        place_of_query = token_col + (exp * tokens_own + t * tile)
        inside = jnp.zeros((head, cols), F32)
        for doc, (start, end) in enumerate(ends):
            here = (place_of_query >= start) & (place_of_query < end) & (extra_row == doc)
            inside = jnp.where(here, 1.0, inside)
        r.qt[t, :head] = query.astype(BF16)
        r.qt[t, head:] = inside.astype(BF16)

    key_in_tile = lax.broadcasted_iota(jnp.int32, (tile, cols), 0)
    token_in_tile = lax.rem(lax.broadcasted_iota(jnp.int32, (tile, cols), 1), tile)
    for t in range(tiles):
        edge = t * tile
        query = r.qt[t]
        last = jnp.where(
            key_in_tile <= token_in_tile,
            dot_nn(r.kx[exp, edge : edge + tile], query),
            MASKED_SCORE,
        )
        top_score = jnp.max(last, axis=0, keepdims=True)
        if t > 0:
            early = dot_nn(r.kx[exp, :edge], query)
            top_score = jnp.maximum(top_score, jnp.max(early, axis=0, keepdims=True))
        weight = jnp.exp(last - top_score)
        total_weight = jnp.sum(weight, axis=0, keepdims=True)
        summed = dot_nn(r.kvt[exp, head:, edge : edge + tile], weight.astype(BF16))
        if t > 0:
            weight = jnp.exp(early - top_score)
            total_weight += jnp.sum(weight, axis=0, keepdims=True)
            summed += dot_nn(r.kvt[exp, head:, :edge], weight.astype(BF16))
        r.peak[t], r.total[t], r.acc[t] = top_score, total_weight, summed

    halves = [slice(half * cols // 2, (half + 1) * cols // 2) for half in range(2)]
    first_turn = jnp.where(near < exp, 0, jnp.where(far < exp, 1, 0))
    end_turn = jnp.where(far < exp, 3, jnp.where(near < exp, 1, 0))

    def score_tile(block, t):
        for half, span in enumerate(halves):
            r.wide[2 * t + half] = dot_nn(r.kx[block], r.qt[t, :, span])

    def sum_tile(block, t):
        for half, span in enumerate(halves):
            scores = r.wide[2 * t + half]
            old = r.peak[t, :, span]
            new = jnp.maximum(old, jnp.max(scores, axis=0, keepdims=True))
            weight = jnp.exp(scores - new)
            fade = jnp.exp(old - new)
            r.peak[t, :, span] = new
            r.total[t, :, span] = r.total[t, :, span] * fade + jnp.sum(
                weight, axis=0, keepdims=True
            )
            r.acc[t, :, span] = r.acc[t, :, span] * fade + dot_nn(
                r.kvt[block, head:], weight.astype(BF16)
            )

    def block_at(turn):
        return jnp.where(turn == 0, near, jnp.where(turn == 1, far, across))

    def arrive(step, block):
        gather_wait(KEYS, step)
        prepare_keys(block)

    def arrive_far():
        arrive(1, far)
        gather_start(OUT)

    def forward_turn(turn, carry):
        block = block_at(turn)
        for t in range(tiles - 1):
            score_tile(block, t + 1)
            sum_tile(block, t)
        pl.when((turn == 0) & (end_turn > 1))(arrive_far)
        pl.when(turn == 1)(functools.partial(arrive, 2, across))
        score_tile(jnp.where(turn + 1 < end_turn, block_at(turn + 1), exp), 0)
        sum_tile(block, tiles - 1)
        return carry

    arrive(0, near)
    pl.when((first_turn == 1) | (end_turn <= 1))(arrive_far)
    pl.when(end_turn <= 1)(functools.partial(arrive, 2, across))
    pl.when(end_turn > 0)(lambda: score_tile(block_at(first_turn), 0))
    lax.fori_loop(first_turn, end_turn, forward_turn, 0)
    for t in range(tiles):
        r.acc[t] = (r.acc[t] / r.total[t]).astype(BF16).astype(F32)
        r.peak[t] = r.peak[t] + jnp.log(r.total[t])

    for t in range(tiles):
        shares = [
            r.acc[t, :, slot * tile : (slot + 1) * tile] * gate_row(slot, t)
            for slot in range(top)
        ]
        for expert in range(all_experts):
            spread = jnp.zeros((head, tile), F32)
            for slot in range(top):
                spread = jnp.where(route_row(slot, t) == expert, shares[slot], spread)
            r.spread[expert * head : (expert + 1) * head, t * tile : (t + 1) * tile] = (
                spread.astype(BF16)
            )
    gather_wait(OUT, 1)
    gather_wait(OUT, 0)
    gather_wait(OUT, 2)
    loads[2].wait()
    wo_flat = r.wo[...].reshape(flat, width)
    r.wide[0] = r.tok[...].astype(F32) + dot_nn(r.spread[...].T, wo_flat)

    mixed = r.wide[0]
    scale_ffn = lax.rsqrt(jnp.mean(mixed * mixed, axis=1, keepdims=True) + NORM_EPSILON)
    r.nf[...] = (mixed * scale_ffn * r.gain_ffn[...]).astype(BF16)
    r.nft[...] = r.nf[...].T
    loads[5].wait()

    stores = []

    def store(source, target):
        def begin():
            copy = pltpu.make_async_copy(source, target, r.store_sem.at[len(stores)])
            stores.append((source, target, len(stores)))
            copy.start()

        return begin

    def store_chunk(chunk):
        span = slice(chunk * FF_CHUNK, (chunk + 1) * FF_CHUNK)
        array = r.ffn[chunk][1]
        first = store(array.at[:FF_CHUNK], r.grad_down.at[span])
        second = store(array.at[FF_CHUNK:], r.grad_up.at[:, span])

        def begin():
            first()
            second()

        return begin

    ffn = [
        Reduction(place, r.ffn[chunk], *FFN_SUMS[chunk], store_chunk(chunk))
        for chunk in range(chunks)
    ]
    red_out = Reduction(place, r.out_sums, *OUT_SUMS, store(r.out_sums[1], r.grad_out))
    half_width = width // 2
    red_query = [
        Reduction(
            place,
            r.query_sums[half],
            *QUERY_SUMS,
            store(
                r.query_sums[half][1],
                r.grad_query.at[:, half * half_width : (half + 1) * half_width],
            ),
        )
        for half in range(2)
    ]
    red_small = Reduction(place, r.small_sums, *SMALL_SUMS, store(r.small_sums[1], r.grad_small))

    def store_by_owner(target, table):
        for block in range(exp_size):
            spot = (block % 2) * 2 + block // 2
            target[spot * expert_rows : (spot + 1) * expert_rows] = table[
                block * expert_rows : (block + 1) * expert_rows
            ].astype(BF16)

    moving = [*ffn, red_out, *red_query, red_small]

    def hook(point):
        for one in SCHEDULE.get(point, ()):
            moving[one].advance()

    root = math.sqrt(2.0 / math.pi)
    for chunk in range(chunks):
        span = slice(chunk * FF_CHUNK, (chunk + 1) * FF_CHUNK)
        hidden = dot_nn(r.nf[...], r.up[:, span])
        grad_active = r.grad_hidden[:, span].astype(F32)
        square = hidden * hidden
        bent = jnp.tanh(root * hidden * (1.0 + 0.044715 * square))
        half = 0.5 * (1.0 + bent)
        active = (hidden * half).astype(BF16)
        slope = half + 0.5 * hidden * (1.0 - bent * bent) * (
            root * (1.0 + 3 * 0.044715 * square)
        )
        grad_hidden = (grad_active * slope).astype(BF16)
        r.ffn[chunk][0][:FF_CHUNK] = dot_nn(active.T, r.cot[...]).astype(BF16)
        r.ffn[chunk][0][FF_CHUNK:] = dot_nn(r.nft[...], grad_hidden).astype(BF16)
        ffn[chunk].advance()
        hook((0, 2 * chunk))
        r.active[:, span] = active
        r.grad_hidden[:, span] = grad_hidden
        hook((0, 2 * chunk + 1))

    mixed = r.wide[0]
    grad_nf = dot_nt(r.grad_hidden[...], r.up[...])
    scale_ffn = lax.rsqrt(jnp.mean(mixed * mixed, axis=1, keepdims=True) + NORM_EPSILON)
    gained = grad_nf * r.gain_ffn[...]
    inner = jnp.mean(gained * mixed, axis=1, keepdims=True)
    grad_gain_ffn = jnp.sum(grad_nf * mixed * scale_ffn, axis=0, keepdims=True)
    grad_mixed = (
        r.cot[...].astype(F32)
        + scale_ffn * gained
        - mixed * (scale_ffn * scale_ffn * scale_ffn * inner)
    )
    r.wide[1] = grad_mixed
    r.gm[...] = grad_mixed.astype(BF16)
    store_by_owner(r.out_sums[0], dot_nn(r.spread[...], r.gm[...]))
    red_out.advance()
    hook((1, 0))

    table = dot_nt(r.wo[...].reshape(flat, width), r.gm[...])
    for t in range(tiles):
        for slot in range(top):
            span = slice(slot * tile, (slot + 1) * tile)
            picked = jnp.zeros((head, tile), F32)
            for expert in range(all_experts):
                picked = jnp.where(
                    route_row(slot, t) == expert,
                    table[expert * head : (expert + 1) * head, t * tile : (t + 1) * tile],
                    picked,
                )
            grad = (picked * gate_row(slot, t)).astype(BF16)
            r.dot[t, head:, span] = grad
            r.dot[t, :head, span] = jnp.zeros((head, tile), BF16)
            r.delta[t, :, span] = jnp.sum(
                grad.astype(F32) * r.acc[t, :, span], axis=0, keepdims=True
            )
        r.rows[t] = jnp.concatenate([r.qt[t, :head], r.dot[t, head:]], axis=0).T
        r.acc[t] = jnp.zeros((head, cols), F32)
    hook((1, 1))

    def backward_piece(t, scores, key_values, keys_t):
        weight = jnp.exp(scores - r.peak[t])
        grad_weight = dot_nn(key_values, r.dot[t])
        grad_scores = (weight * (grad_weight - r.delta[t])).astype(BF16)
        r.acc[t] += dot_nn(keys_t, grad_scores)
        by_keys = dot_nn(grad_scores, r.rows[t])
        by_values = dot_nn(weight.astype(BF16), r.rows[t])
        side = lax.broadcasted_iota(jnp.int32, by_keys.shape, 1)
        return jnp.where(side < head, by_keys, by_values)

    def kv_copy(step):
        target = (near, far, near)[step]
        return pltpu.make_async_remote_copy(
            src_ref=r.gkv_out.at[step],
            dst_ref=r.gkv_in.at[step],
            send_sem=r.gkv_send.at[step],
            recv_sem=r.gkv_recv.at[step],
            device_id=(seq, target),
            device_id_type=pl.DeviceIdType.MESH,
        )

    def send_across():
        r.gkv_out[0] = r.gkv[...].astype(BF16)
        kv_copy(0).start()

    def send_far():
        kv_copy(0).wait_recv()
        r.gkv_out[1] = (r.gkv[...] + r.gkv_in[0].astype(F32)).astype(BF16)
        kv_copy(1).start()

    def send_near():
        r.gkv_out[2] = r.gkv[...].astype(BF16)
        kv_copy(2).start()

    def backward_step(step, carry):
        turn, t = lax.div(step, tiles), lax.rem(step, tiles)
        block = jnp.where(turn == 0, across, jnp.where(turn == 1, far, near))

        @pl.when(t == 0)
        def _():
            r.gkv[...] = jnp.zeros((tokens_own, 2 * head), F32)

        @pl.when(block < exp)
        def _():
            scores = dot_nn(r.kx[block], r.qt[t])
            piece = backward_piece(t, scores, r.kv[block], r.kvt[block, :head])

            r.gkv[...] += piece

        pl.when((step == tiles - 1) & (far_bit == 1))(send_across)
        pl.when((step == 2 * tiles - 1) & (far_bit == 1))(send_far)
        pl.when((step == 3 * tiles - 1) & (near_bit == 1))(send_near)
        for turn_step in range(3 * tiles):
            if (2, turn_step) in SCHEDULE:
                pl.when(step == turn_step)(functools.partial(hook, (2, turn_step)))
        return carry

    lax.fori_loop(0, 3 * tiles, backward_step, 0)

    r.gkv[...] = jnp.zeros((tokens_own, 2 * head), F32)
    for t in range(tiles):
        edge = t * tile
        scores = jnp.where(
            key_in_tile <= token_in_tile,
            dot_nn(r.kx[exp, edge : edge + tile], r.qt[t]),
            MASKED_SCORE,
        )
        r.gkv[edge : edge + tile] += backward_piece(
            t, scores, r.kv[exp, edge : edge + tile], r.kvt[exp, :head, edge : edge + tile]
        )
        if t > 0:
            scores = dot_nn(r.kx[exp, :edge], r.qt[t])
            r.gkv[:edge] += backward_piece(
                t, scores, r.kv[exp, :edge], r.kvt[exp, :head, :edge]
            )
        hook((3, t))

    for t in range(tiles):
        shares = [
            (r.acc[t, :, slot * tile : (slot + 1) * tile] * (1.0 / math.sqrt(head)))
            .astype(BF16)
            .astype(F32)
            for slot in range(top)
        ]
        for expert in range(all_experts):
            spread = jnp.zeros((head, tile), F32)
            for slot in range(top):
                spread = jnp.where(route_row(slot, t) == expert, shares[slot], spread)
            r.spread[expert * head : (expert + 1) * head, t * tile : (t + 1) * tile] = (
                spread.astype(BF16)
            )
    for half in range(2):
        span = slice(half * half_width, (half + 1) * half_width)
        store_by_owner(r.query_sums[half][0], dot_nn(r.spread[...], r.normed[:, span]))
        red_query[half].advance()

    @pl.when(near_bit == 0)
    def _():
        kv_copy(2).wait_recv()
        r.gkv[...] += r.gkv_in[2].astype(F32)

    @pl.when(far_bit == 0)
    def _():
        kv_copy(1).wait_recv()
        r.gkv[...] += r.gkv_in[1].astype(F32)

    grad_kv = r.gkv[...].astype(BF16)
    wq_flat = r.wq[...].reshape(flat, width)
    grad_normed = dot_nn(r.spread[...].T, wq_flat) + dot_nt(grad_kv, r.w_kv[...])
    inputs = r.tok[...].astype(F32)
    scale_attn = lax.rsqrt(jnp.mean(inputs * inputs, axis=1, keepdims=True) + NORM_EPSILON)
    grad_gain_attn = jnp.sum(grad_normed * inputs * scale_attn, axis=0, keepdims=True)
    r.small_sums[0][: 2 * head] = dot_nn(grad_kv.T, r.normed[...]).astype(BF16)
    gain_rows = r.small_sums[0].shape[0] - 2 * head
    which = lax.broadcasted_iota(jnp.int32, (gain_rows, width), 0)
    r.small_sums[0][2 * head :] = jnp.where(
        which == 0, grad_gain_attn, jnp.where(which == 1, grad_gain_ffn, 0.0)
    ).astype(BF16)
    red_small.advance()
    gained = grad_normed * r.gain_attn[...]
    inner = jnp.mean(gained * inputs, axis=1, keepdims=True)
    r.nf[...] = (
        r.wide[1]
        + scale_attn * gained
        - inputs * (scale_attn * scale_attn * scale_attn * inner)
    ).astype(BF16)

    store(r.nf, r.grad_tokens)()
    r.gm[...] = (r.wide[0] + dot_nn(r.active[...], r.down[...])).astype(BF16)
    store(r.gm, r.block_out)()

    for one in LAST_STEPS:
        moving[one].advance()
    while not all(one.done for one in moving):
        for one in moving:
            one.advance()
    for kind in (QUERY, KEYS, OUT):
        for step in range(3):
            if (kind, step) != (QUERY, 1):
                gather_copy(kind, step).wait_send()

    @pl.when(far_bit == 1)
    def _():
        kv_copy(0).wait_send()
        kv_copy(1).wait_send()

    pl.when(near_bit == 1)(lambda: kv_copy(2).wait_send())
    for source, target, number in stores:
        pltpu.make_async_copy(source, target, r.store_sem.at[number]).wait()


def finish_kernel(parts, head, refs_in, refs_out, held, wide, load_sem, store_sem):
    loads = [
        pltpu.make_async_copy(
            refs_in[source].at[pl.ds(first, rows)], held[number], load_sem.at[number]
        )
        for number, (source, first, rows) in enumerate(parts)
    ]
    stores = []
    for load in loads:
        load.start()
    for number, (source, first, rows) in enumerate(parts):
        loads[number].wait()
        result = held[number]
        if source >= 2:
            result = wide[number]
            result[...] = held[number][...].astype(F32)
        if source < len(refs_in) - 1:
            stores.append(
                pltpu.make_async_copy(
                    result, refs_out[source].at[pl.ds(first, rows)], store_sem.at[number]
                )
            )
            stores[-1].start()
        else:
            by_key, gain_attn, gain_ffn = refs_out[source:]
            by_key[...] = result[: 2 * head].T
            gain_attn[...] = result[2 * head : 2 * head + 1]
            gain_ffn[...] = result[2 * head + 1 : 2 * head + 2]
    for store in stores:
        store.wait()


def per_device(
    seq_size,
    exp_size,
    tokens,
    lengths,
    routes,
    gates,
    gain_attn,
    w_kv,
    w_query,
    w_out,
    gain_ffn,
    w_up,
    w_down,
    cotangent,
):
    tokens_own, width = tokens.shape
    top = routes.shape[1]
    local_experts, _, head = w_query.shape
    ff = w_up.shape[1]
    docs = lengths.shape[1]
    tiles = tokens_own // TILE_TOKENS
    cols = top * TILE_TOKENS
    chunks = ff // FF_CHUNK
    expert_rows = local_experts * head
    flat = expert_rows * exp_size
    stages = seq_size.bit_length() - 1 + exp_size.bit_length() - 1
    small_rows = 4 * head
    sizes = (seq_size, exp_size, tokens_own, width, head, top, local_experts, ff, docs)

    vmem = pl.BlockSpec(memory_space=pltpu.VMEM)
    smem = pl.BlockSpec(memory_space=pltpu.SMEM)
    anywhere = pl.BlockSpec(memory_space=pl.ANY)
    inputs = dict(
        lengths=(lengths, smem),
        tokens=(tokens, anywhere),
        routes=(routes.T, vmem),
        gates=(gates.T, vmem),
        gain_attn=(gain_attn.reshape(1, width), vmem),
        w_kv=(w_kv, vmem),
        w_query=(jnp.swapaxes(w_query, 1, 2).reshape(expert_rows, width), anywhere),
        w_out=(w_out.reshape(expert_rows, width), anywhere),
        gain_ffn=(gain_ffn.reshape(1, width), vmem),
        w_up=(w_up, anywhere),
        w_down=(w_down, anywhere),
        cotangent=(cotangent, anywhere),
    )
    outputs = dict(
        block_out=((tokens_own, width), anywhere),
        grad_tokens=((tokens_own, width), anywhere),
        grad_up=((width, ff), anywhere),
        grad_down=((ff, width), anywhere),
        grad_query=((expert_rows, width), anywhere),
        grad_out=((expert_rows, width), anywhere),
        grad_small=((small_rows, width), anywhere),
    )
    scratch = dict(
        up=pltpu.VMEM((width, ff), BF16),
        down=pltpu.VMEM((ff, width), BF16),
        cot=pltpu.VMEM((tokens_own, width), BF16),
        tok=pltpu.VMEM((tokens_own, width), BF16),
        normed=pltpu.VMEM((tokens_own, width), BF16),
        wq=pltpu.VMEM((exp_size, expert_rows, width), BF16),
        wo=pltpu.VMEM((exp_size, expert_rows, width), BF16),
        kv=pltpu.VMEM((exp_size, tokens_own, 2 * head), BF16),
        kx=pltpu.VMEM((exp_size, tokens_own, 2 * head), BF16),
        kvt=pltpu.VMEM((exp_size, 2 * head, tokens_own), BF16),
        qt=pltpu.VMEM((tiles, 2 * head, cols), BF16),
        dot=pltpu.VMEM((tiles, 2 * head, cols), BF16),
        rows=pltpu.VMEM((tiles, cols, 2 * head), BF16),
        acc=pltpu.VMEM((tiles, head, cols), F32),
        peak=pltpu.VMEM((tiles, 1, cols), F32),
        total=pltpu.VMEM((tiles, 1, cols), F32),
        delta=pltpu.VMEM((tiles, 1, cols), F32),
        spread=pltpu.VMEM((flat, tokens_own), BF16),
        wide=pltpu.VMEM((2 * tiles, tokens_own, width), F32),
        nf=pltpu.VMEM((tokens_own, width), BF16),
        nft=pltpu.VMEM((width, tokens_own), BF16),
        active=pltpu.VMEM((tokens_own, ff), BF16),
        grad_hidden=pltpu.VMEM((tokens_own, ff), BF16),
        gm=pltpu.VMEM((tokens_own, width), BF16),
        gkv=pltpu.VMEM((tokens_own, 2 * head), F32),
        gkv_out=pltpu.VMEM((3, tokens_own, 2 * head), BF16),
        gkv_in=pltpu.VMEM((3, tokens_own, 2 * head), BF16),
        load_sem=pltpu.SemaphoreType.DMA((6,)),
        store_sem=pltpu.SemaphoreType.DMA((2 * chunks + 6,)),
        gather_send=pltpu.SemaphoreType.DMA((9,)),
        gather_recv=pltpu.SemaphoreType.DMA((9,)),
        gkv_send=pltpu.SemaphoreType.DMA((3,)),
        gkv_recv=pltpu.SemaphoreType.DMA((3,)),
    )

    def buffers(rows, sums, parts=1):
        return reduction_buffers(rows, width // parts, stages, *sums[1:])

    scratch.update(
        ffn=[buffers(width + FF_CHUNK, FFN_SUMS[chunk]) for chunk in range(chunks)],
        out_sums=buffers(flat, OUT_SUMS),
        query_sums=[buffers(flat, QUERY_SUMS, 2) for _ in range(2)],
        small_sums=buffers(small_rows, SMALL_SUMS),
    )
    scratch_list, scratch_tree = jax.tree.flatten(scratch)

    def kernel(*refs):
        names = [*inputs, *outputs]
        held = jax.tree.unflatten(scratch_tree, refs[len(names) :])
        block_kernel(types.SimpleNamespace(**dict(zip(names, refs)), **held), sizes)

    block_out, grad_tokens, grad_up, grad_down, grad_query, grad_out, small = pl.pallas_call(
        kernel,
        out_shape=[jax.ShapeDtypeStruct(shape, BF16) for shape, _ in outputs.values()],
        in_specs=[spec for _, spec in inputs.values()],
        out_specs=[spec for _, spec in outputs.values()],
        scratch_shapes=scratch_list,
        compiler_params=pltpu.CompilerParams(
            collective_id=0, has_side_effects=True, vmem_limit_bytes=VMEM_LIMIT
        ),
    )(*[array for array, _ in inputs.values()])
    narrow = (block_out, grad_tokens, grad_up, grad_down, grad_query, grad_out, small)
    parts = []
    for number, array in enumerate(narrow):
        pieces = FINISH_PIECES if array.size >= width * ff else 1
        rows = array.shape[0] // pieces
        parts += [(number, piece * rows, rows) for piece in range(pieces)]
    shapes = [(rows, narrow[number].shape[1]) for number, _, rows in parts]
    count = len(narrow)

    def finish(*refs):
        buffers = refs[2 * count + 2 : -2]
        finish_kernel(
            parts,
            head,
            refs[:count],
            refs[count : 2 * count + 2],
            buffers[: len(parts)],
            buffers[len(parts) :],
            *refs[-2:],
        )

    gain = jax.ShapeDtypeStruct((1, width), F32)
    block_out, grad_tokens, grad_up, grad_down, grad_query, grad_out, grad_kv, *gains = (
        pl.pallas_call(
            finish,
            out_shape=[
                jax.ShapeDtypeStruct(array.shape, BF16 if number < 2 else F32)
                for number, array in enumerate(narrow[:-1])
            ]
            + [jax.ShapeDtypeStruct((width, 2 * head), F32), gain, gain],
            in_specs=[anywhere] * count,
            out_specs=[anywhere] * (count - 1) + [vmem] * 3,
            scratch_shapes=[pltpu.VMEM(shape, BF16) for shape in shapes]
            + [pltpu.VMEM(shape, F32) for shape in shapes]
            + [pltpu.SemaphoreType.DMA((len(parts),)) for _ in range(2)],
            compiler_params=pltpu.CompilerParams(vmem_limit_bytes=FINISH_VMEM),
        )(*narrow)
    )
    by_expert = (local_experts, head, width)
    return (
        block_out,
        grad_tokens,
        gains[0].reshape(width),
        grad_kv,
        jnp.swapaxes(grad_query.reshape(by_expert), 1, 2),
        grad_out.reshape(by_expert),
        gains[1].reshape(width),
        grad_up,
        grad_down,
    )


def solution(mesh):
    sizes = dict(mesh.shape)
    return jax.shard_map(
        functools.partial(per_device, sizes["seq"], sizes["exp"]),
        mesh=mesh,
        in_specs=(
            P(("seq", "exp"), None),
            P("seq", None),
            P(("seq", "exp"), None),
            P(("seq", "exp"), None),
            P(),
            P(),
            P("exp", None, None),
            P("exp", None, None),
            P(),
            P(),
            P(),
            P(("seq", "exp"), None),
        ),
        out_specs=(
            P(("seq", "exp"), None),
            P(("seq", "exp"), None),
            P(),
            P(),
            P("exp", None, None),
            P("exp", None, None),
            P(),
            P(),
            P(),
        ),
        check_vma=False,
    )
```

```python
import functools
import math
import types
import typing

import jax
import jax.numpy as jnp
from jax import lax
from jax.experimental import pallas as pl
from jax.experimental.pallas import tpu as pltpu
from jax.sharding import PartitionSpec as P

NORM_EPSILON = 1e-06
MASKED_SCORE = -1e30
TILE_TOKENS = 256
QUERY, KEYS, OUT = range(3)
FF_CHUNK = 512
FINISH_PIECES = 4
FINISH_VMEM = 62 << 20
CORE, Y, X, Z0, Z1 = ((1, 0), (1, 1), (0, 0), (0, 1), (0, 2))
FFN_SUMS = (
    ((CORE, Y, X, Z0, Z1), (1, 2, 2), 0, (1, 2, 2)),
    ((CORE, Y, X, Z0, Z1), (1, 1, 1, 2), 0, (1, 1, 1, 2)),
    ((CORE, X, Z0, Z1, Y), (1, 1, 2, 1), 0, (1, 1, 2, 1)),
    ((CORE, Y, X, Z0, Z1), (1, 2, 2), 0, (1, 1, 1, 2)),
)
OUT_SUMS = ((CORE, Y, X, Z0, Z1), (1, 1, 1, 2), 2, (1, 2))
QUERY_SUMS = ((CORE, Y, X, Z0, Z1), (1, 1, 1, 2), 2, (1, 2))
SMALL_SUMS = ((CORE, Y, X, Z0, Z1), (1, 1, 3), 0, (1, 2, 2))
SCHEDULE = {
    (0, 3): (0,),
    (0, 4): (1,),
    (0, 6): (2,),
    (1, 0): (3,),
    (2, 0): (0, 4),
    (2, 2): (1, 2),
    (2, 3): (0,),
    (2, 4): (3,),
    (2, 6): (1, 4, 2),
    (2, 7): (0,),
    (2, 8): (2, 3, 4),
    (3, 2): (1,),
}
LAST_STEPS = (3, 0, 5, 2, 6, 4, 7, 0, 1, 5, 3, 6, 7, 1, 2, 5, 6, 4, 7, 5, 3, 6, 3, 7, 2, 5, 6, 2, 4, 1, 7, 1, 5, 7, 6)
F32 = jnp.float32
BF16 = jnp.bfloat16
VMEM_LIMIT = 63 << 20


def dot_nn(a, b):
    return jnp.dot(a, b, preferred_element_type=F32)


def dot_nt(a, b):
    return lax.dot_general(a, b, (((1,), (1,)), ((), ())), preferred_element_type=F32)


def index_bit(index, bit):
    return lax.rem(lax.div(index, 1 << bit), 2)


def flip_bit(index, bit):
    return index + (1 << bit) * (1 - 2 * index_bit(index, bit))


def flip(index, mask):
    for bit in range(mask.bit_length()):
        if (mask >> bit) & 1:
            index = flip_bit(index, bit)
    return index


def halving_plan(rows, cols, bits):
    plan = [("x", rows, cols)]
    for _ in range(bits):
        if rows % 32 == 0:
            rows //= 2
            plan.append(("r", rows, cols))
        elif cols % 256 == 0:
            cols //= 2
            plan.append(("c", rows, cols))
        else:
            plan.append(("x", rows, cols))
    return plan


def step_list(rows, cols, bits, groups, keep, back):
    plan = halving_plan(rows, cols, bits)

    def spans(start, sizes):
        found = []
        for size in [*sizes, *([1] * (bits - start - sum(sizes)))]:
            uncut = any(mode == "x" for mode, _, _ in plan[start + 1 : start + size + 1])
            found += [(start + n, start + n + 1) for n in range(size)] if uncut else [(start, start + size)]
            start += size
        return found

    steps = [(False, *span) for span in spans(0, groups)]
    steps += [(True, *span) for span in reversed(spans(keep, back)) if plan[span[1]][0] != "x"]
    return plan, steps


def peer_masks(bits, groups, keep, back):
    found = set()
    for first, sizes in ((0, groups), (keep, back)):
        for size in [*sizes, *([1] * (len(bits) - first - sum(sizes)))]:
            for choice in range(1, 1 << size):
                mask = [0, 0]
                for number in range(size):
                    if (choice >> number) & 1:
                        axis, bit = bits[first + number]
                        mask[axis] |= 1 << bit
                found.add(tuple(mask))
            first += size
    return found


class Place(typing.NamedTuple):
    seq: jax.Array
    exp: jax.Array
    seq_size: int


def with_rest(bits, seq_size):
    return bits + tuple((0, bit) for bit in range(3, seq_size.bit_length() - 1))


class Reduction:
    def __init__(self, place, buffers, bits, groups, keep, back, on_done):
        self.place, self.bits, self.on_done = place, with_rest(bits, place.seq_size), on_done
        self.array, self.final, self.landing, self.send_sem, self.recv_sem = buffers
        rows, cols = self.array.shape
        self.plan, self.steps = step_list(rows, cols, len(self.bits), groups, keep, back)
        self.mine = [index_bit(place[axis], bit) for axis, bit in self.bits]
        span = (0, rows, 0, cols)
        self.spans = [span]
        for number in range(len(self.bits)):
            span = self.part(span, number, self.mine[number])
            self.spans.append(span)
        self.base = self.spans[keep]
        self.first_sem, total = [], 0
        for _, low, high in self.steps:
            self.first_sem.append(total)
            total += (1 << (high - low)) - 1
        self.position = 0
        self.started = False
        self.done = False

    def part(self, span, number, value):
        mode, rows, cols = self.plan[number + 1]
        row_start, _, col_start, _ = span
        if mode == "r":
            row_start = row_start + value * rows
        elif mode == "c":
            col_start = col_start + value * cols
        return (row_start, rows, col_start, cols)

    def final_view(self, span):
        row_start, rows, col_start, cols = span
        return self.view(
            self.final, (row_start - self.base[0], rows, col_start - self.base[2], cols)
        )

    def view(self, ref, span):
        row_start, rows, col_start, cols = span
        index = []
        for start, size, whole in (
            (row_start, rows, ref.shape[0]),
            (col_start, cols, ref.shape[1]),
        ):
            if size == whole:
                index.append(slice(None))
            else:
                index.append(pl.ds(pl.multiple_of(start, math.gcd(size, 512)), size))
        return ref.at[tuple(index)]

    def copy(self, number, mask):
        gathers, low, high = self.steps[number]
        other = list(self.place[:2])
        span = self.spans[low]
        for bit in range(low, high):
            value = self.mine[bit]
            if (mask >> (bit - low)) & 1:
                axis, index = self.bits[bit]
                other[axis] = flip_bit(other[axis], index)
                value = 1 - value
            span = self.part(span, bit, value)
        if gathers:
            source = target = self.final_view(self.spans[high])
        else:
            source, target = self.view(self.array, span), self.landing[number].at[mask - 1]
        slot = self.first_sem[number] + mask - 1
        return pltpu.make_async_remote_copy(
            src_ref=source,
            dst_ref=target,
            send_sem=self.send_sem.at[slot],
            recv_sem=self.recv_sem.at[slot],
            device_id=tuple(other),
            device_id_type=pl.DeviceIdType.MESH,
        )

    def masks(self, number):
        _, low, high = self.steps[number]
        return range(1, 1 << (high - low))

    def in_place(self, number):
        gathers, _, high = self.steps[number]
        return not gathers and self.plan[high][0] == "x"

    def advance(self):
        if self.done:
            return
        number = self.position
        if self.started:
            gathers, _, high = self.steps[number]
            for mask in self.masks(number):
                self.copy(number, mask).wait_recv()
                if self.in_place(number):
                    self.copy(number, mask).wait_send()
            if not gathers:
                kept = self.view(self.array, self.spans[high])
                total = kept[...].astype(F32)
                for mask in self.masks(number):
                    total += self.landing[number][mask - 1].astype(F32)
                if high == len(self.bits):
                    kept = self.final_view(self.spans[high])
                kept[...] = total.astype(BF16)
            self.position += 1
        number = self.position
        if number < len(self.steps):
            for mask in self.masks(number):
                self.copy(number, mask).start()
            self.started = True
        else:
            for number in range(len(self.steps)):
                if not self.in_place(number):
                    for mask in self.masks(number):
                        self.copy(number, mask).wait_send()
            self.done = True
            self.on_done()


def reduction_buffers(rows, cols, bits, groups, keep, back):
    plan, steps = step_list(rows, cols, bits, groups, keep, back)
    held_rows, held_cols = plan[keep][1:]
    landing = [
        pltpu.VMEM(((1 << (high - low)) - 1, *plan[high][1:]), BF16)
        for gathers, low, high in steps
        if not gathers
    ]
    slots = sum((1 << (high - low)) - 1 for _, low, high in steps)
    sems = pltpu.SemaphoreType.DMA((slots,))
    return [pltpu.VMEM((rows, cols), BF16), pltpu.VMEM((held_rows, held_cols), BF16), landing, sems, sems]


def block_kernel(r, sizes):
    seq_size, exp_size, tokens_own, width, head, top, local_experts, ff, docs = sizes
    all_experts = local_experts * exp_size
    expert_rows = local_experts * head
    flat = all_experts * head
    tile = TILE_TOKENS
    tiles = tokens_own // tile
    cols = top * tile
    chunks = ff // FF_CHUNK
    seq, exp = lax.axis_index("seq"), lax.axis_index("exp")
    place = Place(seq, exp, seq_size)
    near, far = flip_bit(exp, 0), flip_bit(exp, 1)
    across = flip_bit(near, 1)
    near_bit, far_bit = index_bit(exp, 0), index_bit(exp, 1)

    barrier = pltpu.get_barrier_semaphore()
    links = {(0, 1), (0, 2)}
    for sums in (*FFN_SUMS, OUT_SUMS, QUERY_SUMS, SMALL_SUMS):
        links |= peer_masks(with_rest(sums[0], seq_size), *sums[1:])
    partners = [(flip(seq, seq_mask), flip(exp, exp_mask)) for seq_mask, exp_mask in sorted(links)]
    for partner in partners:
        pl.semaphore_signal(
            barrier, inc=1, device_id=partner, device_id_type=pl.DeviceIdType.MESH
        )

    arrays = (
        (r.tokens, r.tok),
        (r.w_query, r.wq.at[exp]),
        (r.w_out, r.wo.at[exp]),
        (r.cotangent, r.cot),
        (r.w_down, r.down),
        (r.w_up, r.up),
    )
    loads = [
        pltpu.make_async_copy(source, target, r.load_sem.at[number])
        for number, (source, target) in enumerate(arrays)
    ]
    for load in loads:
        load.start()
    loads[0].wait()

    inputs = r.tok[...].astype(F32)
    scale_attn = lax.rsqrt(jnp.mean(inputs * inputs, axis=1, keepdims=True) + NORM_EPSILON)
    r.normed[...] = (inputs * scale_attn * r.gain_attn[...]).astype(BF16)
    r.kv[exp] = dot_nn(r.normed[...], r.w_kv[...]).astype(BF16)
    pl.semaphore_wait(barrier, len(partners))

    def gather_copy(kind, step):
        block, target = ((exp, near), (exp, far), (far, near))[step]
        number = kind * 3 + step
        blocks = (r.wq, r.kv, r.wo)[kind]
        own = (r.w_query, r.kv.at[exp], r.w_out)[kind]
        return pltpu.make_async_remote_copy(
            src_ref=own if step < 2 else blocks.at[block],
            dst_ref=blocks.at[block],
            send_sem=r.gather_send.at[number],
            recv_sem=r.gather_recv.at[number],
            device_id=(seq, target),
            device_id_type=pl.DeviceIdType.MESH,
        )

    def gather_start(kind):
        gather_copy(kind, 1).start()
        gather_copy(kind, 0).start()

    def gather_wait(kind, step):
        gather_copy(kind, step).wait_recv()
        if step == 1:
            gather_copy(kind, 2).start()

    gather_start(QUERY)

    def route_row(slot, t):
        return r.routes[slot : slot + 1, t * tile : (t + 1) * tile]

    def gate_row(slot, t):
        return r.gates[slot : slot + 1, t * tile : (t + 1) * tile]

    def add_queries(block, first):
        table = dot_nt(r.wq[block], r.normed[...])
        for t in range(tiles):
            part = table[:, t * tile : (t + 1) * tile]
            for slot in range(top):
                span = slice(slot * tile, (slot + 1) * tile)
                picked = jnp.zeros((head, tile), F32) if first else r.acc[t, :, span]
                for local in range(local_experts):
                    picked = jnp.where(
                        route_row(slot, t) == block * local_experts + local,
                        part[local * head : (local + 1) * head],
                        picked,
                    )
                r.acc[t, :, span] = picked

    loads[1].wait()
    add_queries(exp, True)

    ends, total = [], jnp.int32(0)
    for doc in range(docs):
        start, total = total, total + r.lengths[0, doc]
        ends.append((start, total))
    lane = lax.broadcasted_iota(jnp.int32, (tokens_own, 2 * head), 1)
    row = lax.broadcasted_iota(jnp.int32, (tokens_own, 2 * head), 0)

    def prepare_keys(block):
        block_kv = r.kv[block]
        place_of_key = row + block * tokens_own
        extra = jnp.zeros((tokens_own, 2 * head), F32)
        for doc, (start, end) in enumerate(ends):
            outside = (place_of_key < start) | (place_of_key >= end)
            extra = jnp.where((lane == head + doc) & outside, MASKED_SCORE, extra)
        r.kx[block] = jnp.where(lane < head, block_kv.astype(F32), extra).astype(BF16)
        r.kvt[block] = block_kv.T

    prepare_keys(exp)

    gather_wait(QUERY, 0)
    add_queries(near, False)

    loads[3].wait()
    loads[4].wait()
    for chunk in range(chunks):
        span = slice(chunk * FF_CHUNK, (chunk + 1) * FF_CHUNK)
        r.grad_hidden[:, span] = dot_nt(r.cot[...], r.down[span]).astype(BF16)
    gather_copy(QUERY, 1).wait_send()
    gather_start(KEYS)
    gather_wait(QUERY, 1)
    add_queries(far, False)
    gather_wait(QUERY, 2)
    add_queries(across, False)
    extra_row = lax.broadcasted_iota(jnp.int32, (head, cols), 0)
    token_col = lax.rem(lax.broadcasted_iota(jnp.int32, (head, cols), 1), tile)
    for t in range(tiles):
        query = r.acc[t].astype(BF16).astype(F32) * (1.0 / math.sqrt(head))
        place_of_query = token_col + (exp * tokens_own + t * tile)
        inside = jnp.zeros((head, cols), F32)
        for doc, (start, end) in enumerate(ends):
            here = (place_of_query >= start) & (place_of_query < end) & (extra_row == doc)
            inside = jnp.where(here, 1.0, inside)
        r.qt[t, :head] = query.astype(BF16)
        r.qt[t, head:] = inside.astype(BF16)

    key_in_tile = lax.broadcasted_iota(jnp.int32, (tile, cols), 0)
    token_in_tile = lax.rem(lax.broadcasted_iota(jnp.int32, (tile, cols), 1), tile)
    for t in range(tiles):
        edge = t * tile
        query = r.qt[t]
        last = jnp.where(
            key_in_tile <= token_in_tile,
            dot_nn(r.kx[exp, edge : edge + tile], query),
            MASKED_SCORE,
        )
        top_score = jnp.max(last, axis=0, keepdims=True)
        if t > 0:
            early = dot_nn(r.kx[exp, :edge], query)
            top_score = jnp.maximum(top_score, jnp.max(early, axis=0, keepdims=True))
        weight = jnp.exp(last - top_score)
        total_weight = jnp.sum(weight, axis=0, keepdims=True)
        summed = dot_nn(r.kvt[exp, head:, edge : edge + tile], weight.astype(BF16))
        if t > 0:
            weight = jnp.exp(early - top_score)
            total_weight += jnp.sum(weight, axis=0, keepdims=True)
            summed += dot_nn(r.kvt[exp, head:, :edge], weight.astype(BF16))
        r.peak[t], r.total[t], r.acc[t] = top_score, total_weight, summed

    halves = [slice(half * cols // 2, (half + 1) * cols // 2) for half in range(2)]
    first_turn = jnp.where(near < exp, 0, jnp.where(far < exp, 1, 0))
    end_turn = jnp.where(far < exp, 3, jnp.where(near < exp, 1, 0))

    def score_tile(block, t):
        for half, span in enumerate(halves):
            r.wide[2 * t + half] = dot_nn(r.kx[block], r.qt[t, :, span])

    def sum_tile(block, t):
        for half, span in enumerate(halves):
            scores = r.wide[2 * t + half]
            old = r.peak[t, :, span]
            new = jnp.maximum(old, jnp.max(scores, axis=0, keepdims=True))
            weight = jnp.exp(scores - new)
            fade = jnp.exp(old - new)
            r.peak[t, :, span] = new
            r.total[t, :, span] = r.total[t, :, span] * fade + jnp.sum(
                weight, axis=0, keepdims=True
            )
            r.acc[t, :, span] = r.acc[t, :, span] * fade + dot_nn(
                r.kvt[block, head:], weight.astype(BF16)
            )

    def block_at(turn):
        return jnp.where(turn == 0, near, jnp.where(turn == 1, far, across))

    def arrive(step, block):
        gather_wait(KEYS, step)
        prepare_keys(block)

    def arrive_far():
        arrive(1, far)
        gather_start(OUT)

    def forward_turn(turn, carry):
        block = block_at(turn)
        for t in range(tiles - 1):
            score_tile(block, t + 1)
            sum_tile(block, t)
        pl.when((turn == 0) & (end_turn > 1))(arrive_far)
        pl.when(turn == 1)(functools.partial(arrive, 2, across))
        score_tile(jnp.where(turn + 1 < end_turn, block_at(turn + 1), exp), 0)
        sum_tile(block, tiles - 1)
        return carry

    arrive(0, near)
    pl.when((first_turn == 1) | (end_turn <= 1))(arrive_far)
    pl.when(end_turn <= 1)(functools.partial(arrive, 2, across))
    pl.when(end_turn > 0)(lambda: score_tile(block_at(first_turn), 0))
    lax.fori_loop(first_turn, end_turn, forward_turn, 0)
    for t in range(tiles):
        r.acc[t] = (r.acc[t] / r.total[t]).astype(BF16).astype(F32)
        r.peak[t] = r.peak[t] + jnp.log(r.total[t])

    for t in range(tiles):
        shares = [
            r.acc[t, :, slot * tile : (slot + 1) * tile] * gate_row(slot, t)
            for slot in range(top)
        ]
        for expert in range(all_experts):
            spread = jnp.zeros((head, tile), F32)
            for slot in range(top):
                spread = jnp.where(route_row(slot, t) == expert, shares[slot], spread)
            r.spread[expert * head : (expert + 1) * head, t * tile : (t + 1) * tile] = (
                spread.astype(BF16)
            )
    gather_wait(OUT, 1)
    gather_wait(OUT, 0)
    gather_wait(OUT, 2)
    loads[2].wait()
    wo_flat = r.wo[...].reshape(flat, width)
    r.wide[0] = r.tok[...].astype(F32) + dot_nn(r.spread[...].T, wo_flat)

    mixed = r.wide[0]
    scale_ffn = lax.rsqrt(jnp.mean(mixed * mixed, axis=1, keepdims=True) + NORM_EPSILON)
    r.nf[...] = (mixed * scale_ffn * r.gain_ffn[...]).astype(BF16)
    r.nft[...] = r.nf[...].T
    loads[5].wait()

    stores = []

    def store(source, target):
        def begin():
            copy = pltpu.make_async_copy(source, target, r.store_sem.at[len(stores)])
            stores.append((source, target, len(stores)))
            copy.start()

        return begin

    def store_chunk(chunk):
        span = slice(chunk * FF_CHUNK, (chunk + 1) * FF_CHUNK)
        array = r.ffn[chunk][1]
        first = store(array.at[:FF_CHUNK], r.grad_down.at[span])
        second = store(array.at[FF_CHUNK:], r.grad_up.at[:, span])

        def begin():
            first()
            second()

        return begin

    ffn = [
        Reduction(place, r.ffn[chunk], *FFN_SUMS[chunk], store_chunk(chunk))
        for chunk in range(chunks)
    ]
    red_out = Reduction(place, r.out_sums, *OUT_SUMS, store(r.out_sums[1], r.grad_out))
    half_width = width // 2
    red_query = [
        Reduction(
            place,
            r.query_sums[half],
            *QUERY_SUMS,
            store(
                r.query_sums[half][1],
                r.grad_query.at[:, half * half_width : (half + 1) * half_width],
            ),
        )
        for half in range(2)
    ]
    red_small = Reduction(place, r.small_sums, *SMALL_SUMS, store(r.small_sums[1], r.grad_small))

    def store_by_owner(target, table):
        for block in range(exp_size):
            spot = (block % 2) * 2 + block // 2
            target[spot * expert_rows : (spot + 1) * expert_rows] = table[
                block * expert_rows : (block + 1) * expert_rows
            ].astype(BF16)

    moving = [*ffn, red_out, *red_query, red_small]

    def hook(point):
        for one in SCHEDULE.get(point, ()):
            moving[one].advance()

    root = math.sqrt(2.0 / math.pi)
    for chunk in range(chunks):
        span = slice(chunk * FF_CHUNK, (chunk + 1) * FF_CHUNK)
        hidden = dot_nn(r.nf[...], r.up[:, span])
        grad_active = r.grad_hidden[:, span].astype(F32)
        square = hidden * hidden
        bent = jnp.tanh(root * hidden * (1.0 + 0.044715 * square))
        half = 0.5 * (1.0 + bent)
        active = (hidden * half).astype(BF16)
        slope = half + 0.5 * hidden * (1.0 - bent * bent) * (
            root * (1.0 + 3 * 0.044715 * square)
        )
        grad_hidden = (grad_active * slope).astype(BF16)
        r.ffn[chunk][0][:FF_CHUNK] = dot_nn(active.T, r.cot[...]).astype(BF16)
        r.ffn[chunk][0][FF_CHUNK:] = dot_nn(r.nft[...], grad_hidden).astype(BF16)
        ffn[chunk].advance()
        hook((0, 2 * chunk))
        r.active[:, span] = active
        r.grad_hidden[:, span] = grad_hidden
        hook((0, 2 * chunk + 1))

    mixed = r.wide[0]
    grad_nf = dot_nt(r.grad_hidden[...], r.up[...])
    scale_ffn = lax.rsqrt(jnp.mean(mixed * mixed, axis=1, keepdims=True) + NORM_EPSILON)
    gained = grad_nf * r.gain_ffn[...]
    inner = jnp.mean(gained * mixed, axis=1, keepdims=True)
    grad_gain_ffn = jnp.sum(grad_nf * mixed * scale_ffn, axis=0, keepdims=True)
    grad_mixed = (
        r.cot[...].astype(F32)
        + scale_ffn * gained
        - mixed * (scale_ffn * scale_ffn * scale_ffn * inner)
    )
    r.wide[1] = grad_mixed
    r.gm[...] = grad_mixed.astype(BF16)
    store_by_owner(r.out_sums[0], dot_nn(r.spread[...], r.gm[...]))
    red_out.advance()
    hook((1, 0))

    table = dot_nt(r.wo[...].reshape(flat, width), r.gm[...])
    for t in range(tiles):
        for slot in range(top):
            span = slice(slot * tile, (slot + 1) * tile)
            picked = jnp.zeros((head, tile), F32)
            for expert in range(all_experts):
                picked = jnp.where(
                    route_row(slot, t) == expert,
                    table[expert * head : (expert + 1) * head, t * tile : (t + 1) * tile],
                    picked,
                )
            grad = (picked * gate_row(slot, t)).astype(BF16)
            r.dot[t, head:, span] = grad
            r.dot[t, :head, span] = jnp.zeros((head, tile), BF16)
            r.delta[t, :, span] = jnp.sum(
                grad.astype(F32) * r.acc[t, :, span], axis=0, keepdims=True
            )
        r.rows[t] = jnp.concatenate([r.qt[t, :head], r.dot[t, head:]], axis=0).T
        r.acc[t] = jnp.zeros((head, cols), F32)
    hook((1, 1))

    def backward_piece(t, scores, key_values, keys_t):
        weight = jnp.exp(scores - r.peak[t])
        grad_weight = dot_nn(key_values, r.dot[t])
        grad_scores = (weight * (grad_weight - r.delta[t])).astype(BF16)
        r.acc[t] += dot_nn(keys_t, grad_scores)
        by_keys = dot_nn(grad_scores, r.rows[t])
        by_values = dot_nn(weight.astype(BF16), r.rows[t])
        side = lax.broadcasted_iota(jnp.int32, by_keys.shape, 1)
        return jnp.where(side < head, by_keys, by_values)

    def kv_copy(step):
        target = (near, far, near)[step]
        return pltpu.make_async_remote_copy(
            src_ref=r.gkv_out.at[step],
            dst_ref=r.gkv_in.at[step],
            send_sem=r.gkv_send.at[step],
            recv_sem=r.gkv_recv.at[step],
            device_id=(seq, target),
            device_id_type=pl.DeviceIdType.MESH,
        )

    def send_across():
        r.gkv_out[0] = r.gkv[...].astype(BF16)
        kv_copy(0).start()

    def send_far():
        kv_copy(0).wait_recv()
        r.gkv_out[1] = (r.gkv[...] + r.gkv_in[0].astype(F32)).astype(BF16)
        kv_copy(1).start()

    def send_near():
        r.gkv_out[2] = r.gkv[...].astype(BF16)
        kv_copy(2).start()

    def backward_step(step, carry):
        turn, t = lax.div(step, tiles), lax.rem(step, tiles)
        block = jnp.where(turn == 0, across, jnp.where(turn == 1, far, near))

        @pl.when(t == 0)
        def _():
            r.gkv[...] = jnp.zeros((tokens_own, 2 * head), F32)

        @pl.when(block < exp)
        def _():
            scores = dot_nn(r.kx[block], r.qt[t])
            piece = backward_piece(t, scores, r.kv[block], r.kvt[block, :head])

            r.gkv[...] += piece

        pl.when((step == tiles - 1) & (far_bit == 1))(send_across)
        pl.when((step == 2 * tiles - 1) & (far_bit == 1))(send_far)
        pl.when((step == 3 * tiles - 1) & (near_bit == 1))(send_near)
        for turn_step in range(3 * tiles):
            if (2, turn_step) in SCHEDULE:
                pl.when(step == turn_step)(functools.partial(hook, (2, turn_step)))
        return carry

    lax.fori_loop(0, 3 * tiles, backward_step, 0)

    r.gkv[...] = jnp.zeros((tokens_own, 2 * head), F32)
    for t in range(tiles):
        edge = t * tile
        scores = jnp.where(
            key_in_tile <= token_in_tile,
            dot_nn(r.kx[exp, edge : edge + tile], r.qt[t]),
            MASKED_SCORE,
        )
        r.gkv[edge : edge + tile] += backward_piece(
            t, scores, r.kv[exp, edge : edge + tile], r.kvt[exp, :head, edge : edge + tile]
        )
        if t > 0:
            scores = dot_nn(r.kx[exp, :edge], r.qt[t])
            r.gkv[:edge] += backward_piece(
                t, scores, r.kv[exp, :edge], r.kvt[exp, :head, :edge]
            )
        hook((3, t))

    for t in range(tiles):
        shares = [
            (r.acc[t, :, slot * tile : (slot + 1) * tile] * (1.0 / math.sqrt(head)))
            .astype(BF16)
            .astype(F32)
            for slot in range(top)
        ]
        for expert in range(all_experts):
            spread = jnp.zeros((head, tile), F32)
            for slot in range(top):
                spread = jnp.where(route_row(slot, t) == expert, shares[slot], spread)
            r.spread[expert * head : (expert + 1) * head, t * tile : (t + 1) * tile] = (
                spread.astype(BF16)
            )
    for half in range(2):
        span = slice(half * half_width, (half + 1) * half_width)
        store_by_owner(r.query_sums[half][0], dot_nn(r.spread[...], r.normed[:, span]))
        red_query[half].advance()

    @pl.when(near_bit == 0)
    def _():
        kv_copy(2).wait_recv()
        r.gkv[...] += r.gkv_in[2].astype(F32)

    @pl.when(far_bit == 0)
    def _():
        kv_copy(1).wait_recv()
        r.gkv[...] += r.gkv_in[1].astype(F32)

    grad_kv = r.gkv[...].astype(BF16)
    wq_flat = r.wq[...].reshape(flat, width)
    grad_normed = dot_nn(r.spread[...].T, wq_flat) + dot_nt(grad_kv, r.w_kv[...])
    inputs = r.tok[...].astype(F32)
    scale_attn = lax.rsqrt(jnp.mean(inputs * inputs, axis=1, keepdims=True) + NORM_EPSILON)
    grad_gain_attn = jnp.sum(grad_normed * inputs * scale_attn, axis=0, keepdims=True)
    r.small_sums[0][: 2 * head] = dot_nn(grad_kv.T, r.normed[...]).astype(BF16)
    gain_rows = r.small_sums[0].shape[0] - 2 * head
    which = lax.broadcasted_iota(jnp.int32, (gain_rows, width), 0)
    r.small_sums[0][2 * head :] = jnp.where(
        which == 0, grad_gain_attn, jnp.where(which == 1, grad_gain_ffn, 0.0)
    ).astype(BF16)
    red_small.advance()
    gained = grad_normed * r.gain_attn[...]
    inner = jnp.mean(gained * inputs, axis=1, keepdims=True)
    r.nf[...] = (
        r.wide[1]
        + scale_attn * gained
        - inputs * (scale_attn * scale_attn * scale_attn * inner)
    ).astype(BF16)

    store(r.nf, r.grad_tokens)()
    r.gm[...] = (r.wide[0] + dot_nn(r.active[...], r.down[...])).astype(BF16)
    store(r.gm, r.block_out)()

    for one in LAST_STEPS:
        moving[one].advance()
    while not all(one.done for one in moving):
        for one in moving:
            one.advance()
    for kind in (QUERY, KEYS, OUT):
        for step in range(3):
            if (kind, step) != (QUERY, 1):
                gather_copy(kind, step).wait_send()

    @pl.when(far_bit == 1)
    def _():
        kv_copy(0).wait_send()
        kv_copy(1).wait_send()

    pl.when(near_bit == 1)(lambda: kv_copy(2).wait_send())
    for source, target, number in stores:
        pltpu.make_async_copy(source, target, r.store_sem.at[number]).wait()


def finish_kernel(parts, head, refs_in, refs_out, held, wide, load_sem, store_sem):
    loads = [
        pltpu.make_async_copy(
            refs_in[source].at[pl.ds(first, rows)], held[number], load_sem.at[number]
        )
        for number, (source, first, rows) in enumerate(parts)
    ]
    stores = []
    for load in loads:
        load.start()
    for number, (source, first, rows) in enumerate(parts):
        loads[number].wait()
        result = held[number]
        if source >= 2:
            result = wide[number]
            result[...] = held[number][...].astype(F32)
        if source < len(refs_in) - 1:
            stores.append(
                pltpu.make_async_copy(
                    result, refs_out[source].at[pl.ds(first, rows)], store_sem.at[number]
                )
            )
            stores[-1].start()
        else:
            by_key, gain_attn, gain_ffn = refs_out[source:]
            by_key[...] = result[: 2 * head].T
            gain_attn[...] = result[2 * head : 2 * head + 1]
            gain_ffn[...] = result[2 * head + 1 : 2 * head + 2]
    for store in stores:
        store.wait()


def per_device(
    seq_size,
    exp_size,
    tokens,
    lengths,
    routes,
    gates,
    gain_attn,
    w_kv,
    w_query,
    w_out,
    gain_ffn,
    w_up,
    w_down,
    cotangent,
):
    tokens_own, width = tokens.shape
    top = routes.shape[1]
    local_experts, _, head = w_query.shape
    ff = w_up.shape[1]
    docs = lengths.shape[1]
    tiles = tokens_own // TILE_TOKENS
    cols = top * TILE_TOKENS
    chunks = ff // FF_CHUNK
    expert_rows = local_experts * head
    flat = expert_rows * exp_size
    stages = seq_size.bit_length() - 1 + exp_size.bit_length() - 1
    small_rows = 4 * head
    sizes = (seq_size, exp_size, tokens_own, width, head, top, local_experts, ff, docs)

    vmem = pl.BlockSpec(memory_space=pltpu.VMEM)
    smem = pl.BlockSpec(memory_space=pltpu.SMEM)
    anywhere = pl.BlockSpec(memory_space=pl.ANY)
    inputs = dict(
        lengths=(lengths, smem),
        tokens=(tokens, anywhere),
        routes=(routes.T, vmem),
        gates=(gates.T, vmem),
        gain_attn=(gain_attn.reshape(1, width), vmem),
        w_kv=(w_kv, vmem),
        w_query=(jnp.swapaxes(w_query, 1, 2).reshape(expert_rows, width), anywhere),
        w_out=(w_out.reshape(expert_rows, width), anywhere),
        gain_ffn=(gain_ffn.reshape(1, width), vmem),
        w_up=(w_up, anywhere),
        w_down=(w_down, anywhere),
        cotangent=(cotangent, anywhere),
    )
    outputs = dict(
        block_out=((tokens_own, width), anywhere),
        grad_tokens=((tokens_own, width), anywhere),
        grad_up=((width, ff), anywhere),
        grad_down=((ff, width), anywhere),
        grad_query=((expert_rows, width), anywhere),
        grad_out=((expert_rows, width), anywhere),
        grad_small=((small_rows, width), anywhere),
    )
    scratch = dict(
        up=pltpu.VMEM((width, ff), BF16),
        down=pltpu.VMEM((ff, width), BF16),
        cot=pltpu.VMEM((tokens_own, width), BF16),
        tok=pltpu.VMEM((tokens_own, width), BF16),
        normed=pltpu.VMEM((tokens_own, width), BF16),
        wq=pltpu.VMEM((exp_size, expert_rows, width), BF16),
        wo=pltpu.VMEM((exp_size, expert_rows, width), BF16),
        kv=pltpu.VMEM((exp_size, tokens_own, 2 * head), BF16),
        kx=pltpu.VMEM((exp_size, tokens_own, 2 * head), BF16),
        kvt=pltpu.VMEM((exp_size, 2 * head, tokens_own), BF16),
        qt=pltpu.VMEM((tiles, 2 * head, cols), BF16),
        dot=pltpu.VMEM((tiles, 2 * head, cols), BF16),
        rows=pltpu.VMEM((tiles, cols, 2 * head), BF16),
        acc=pltpu.VMEM((tiles, head, cols), F32),
        peak=pltpu.VMEM((tiles, 1, cols), F32),
        total=pltpu.VMEM((tiles, 1, cols), F32),
        delta=pltpu.VMEM((tiles, 1, cols), F32),
        spread=pltpu.VMEM((flat, tokens_own), BF16),
        wide=pltpu.VMEM((2 * tiles, tokens_own, width), F32),
        nf=pltpu.VMEM((tokens_own, width), BF16),
        nft=pltpu.VMEM((width, tokens_own), BF16),
        active=pltpu.VMEM((tokens_own, ff), BF16),
        grad_hidden=pltpu.VMEM((tokens_own, ff), BF16),
        gm=pltpu.VMEM((tokens_own, width), BF16),
        gkv=pltpu.VMEM((tokens_own, 2 * head), F32),
        gkv_out=pltpu.VMEM((3, tokens_own, 2 * head), BF16),
        gkv_in=pltpu.VMEM((3, tokens_own, 2 * head), BF16),
        load_sem=pltpu.SemaphoreType.DMA((6,)),
        store_sem=pltpu.SemaphoreType.DMA((2 * chunks + 6,)),
        gather_send=pltpu.SemaphoreType.DMA((9,)),
        gather_recv=pltpu.SemaphoreType.DMA((9,)),
        gkv_send=pltpu.SemaphoreType.DMA((3,)),
        gkv_recv=pltpu.SemaphoreType.DMA((3,)),
    )

    def buffers(rows, sums, parts=1):
        return reduction_buffers(rows, width // parts, stages, *sums[1:])

    scratch.update(
        ffn=[buffers(width + FF_CHUNK, FFN_SUMS[chunk]) for chunk in range(chunks)],
        out_sums=buffers(flat, OUT_SUMS),
        query_sums=[buffers(flat, QUERY_SUMS, 2) for _ in range(2)],
        small_sums=buffers(small_rows, SMALL_SUMS),
    )
    scratch_list, scratch_tree = jax.tree.flatten(scratch)

    def kernel(*refs):
        names = [*inputs, *outputs]
        held = jax.tree.unflatten(scratch_tree, refs[len(names) :])
        block_kernel(types.SimpleNamespace(**dict(zip(names, refs)), **held), sizes)

    block_out, grad_tokens, grad_up, grad_down, grad_query, grad_out, small = pl.pallas_call(
        kernel,
        out_shape=[jax.ShapeDtypeStruct(shape, BF16) for shape, _ in outputs.values()],
        in_specs=[spec for _, spec in inputs.values()],
        out_specs=[spec for _, spec in outputs.values()],
        scratch_shapes=scratch_list,
        compiler_params=pltpu.CompilerParams(
            collective_id=0, has_side_effects=True, vmem_limit_bytes=VMEM_LIMIT
        ),
    )(*[array for array, _ in inputs.values()])
    narrow = (block_out, grad_tokens, grad_up, grad_down, grad_query, grad_out, small)
    parts = []
    for number, array in enumerate(narrow):
        pieces = FINISH_PIECES if array.size >= width * ff else 1
        rows = array.shape[0] // pieces
        parts += [(number, piece * rows, rows) for piece in range(pieces)]
    shapes = [(rows, narrow[number].shape[1]) for number, _, rows in parts]
    count = len(narrow)

    def finish(*refs):
        buffers = refs[2 * count + 2 : -2]
        finish_kernel(
            parts,
            head,
            refs[:count],
            refs[count : 2 * count + 2],
            buffers[: len(parts)],
            buffers[len(parts) :],
            *refs[-2:],
        )

    gain = jax.ShapeDtypeStruct((1, width), F32)
    block_out, grad_tokens, grad_up, grad_down, grad_query, grad_out, grad_kv, *gains = (
        pl.pallas_call(
            finish,
            out_shape=[
                jax.ShapeDtypeStruct(array.shape, BF16 if number < 2 else F32)
                for number, array in enumerate(narrow[:-1])
            ]
            + [jax.ShapeDtypeStruct((width, 2 * head), F32), gain, gain],
            in_specs=[anywhere] * count,
            out_specs=[anywhere] * (count - 1) + [vmem] * 3,
            scratch_shapes=[pltpu.VMEM(shape, BF16) for shape in shapes]
            + [pltpu.VMEM(shape, F32) for shape in shapes]
            + [pltpu.SemaphoreType.DMA((len(parts),)) for _ in range(2)],
            compiler_params=pltpu.CompilerParams(vmem_limit_bytes=FINISH_VMEM),
        )(*narrow)
    )
    by_expert = (local_experts, head, width)
    return (
        block_out,
        grad_tokens,
        gains[0].reshape(width),
        grad_kv,
        jnp.swapaxes(grad_query.reshape(by_expert), 1, 2),
        grad_out.reshape(by_expert),
        gains[1].reshape(width),
        grad_up,
        grad_down,
    )


def solution(mesh):
    sizes = dict(mesh.shape)
    return jax.shard_map(
        functools.partial(per_device, sizes["seq"], sizes["exp"]),
        mesh=mesh,
        in_specs=(
            P(("seq", "exp"), None),
            P("seq", None),
            P(("seq", "exp"), None),
            P(("seq", "exp"), None),
            P(),
            P(),
            P("exp", None, None),
            P("exp", None, None),
            P(),
            P(),
            P(),
            P(("seq", "exp"), None),
        ),
        out_specs=(
            P(("seq", "exp"), None),
            P(("seq", "exp"), None),
            P(),
            P(),
            P("exp", None, None),
            P("exp", None, None),
            P(),
            P(),
            P(),
        ),
        check_vma=False,
    )
```
